32 devices in a mesh: row: 4 (over y, x), col: 8 (over z, core).
Axes of the slice: x: 2, y: 2, z: 4, core: 2. Of those that a mesh axis runs over, the one named last changes fastest.
Arguments:
- start_block: float32 [8192, 128], P(('row', 'col')), may hold values from -6 to 6
- vertex_scale: float32 [8192], P(('row', 'col')), may hold values from 0.022097087 to 0.088388346
- adj_tiles: bfloat16 [4, 8, 64, 128, 128], P('row', 'col'), may hold values from 0 to 1
- tile_row: int32 [4, 8, 64], P('row', 'col'), may hold values from 0 to 7
- tile_col: int32 [4, 8, 64], P('row', 'col'), may hold values from 0 to 15
- live_count: int32 [4, 8], P('row', 'col'), may hold values from 16 to 64, as said below
- rotation_first: float32 [256, 128], replicated, may hold values from -0.375 to 0.375
- rotation_second: float32 [384, 128], replicated, may hold values from -0.3125 to 0.3125
Outputs:
- final_block: float32 [8192, 128], P(('row', 'col'))
- final_image: float32 [8192, 128], P(('row', 'col'))
The draws below stay inside these ranges and needn't reach their ends.
Inputs may be any that keep to these rules, and one draw needn't show every extreme that they name: Slots from live_count on are ignored; at least one device has all 64 slots live in every draw.
All inputs are finite; a program needn't handle non-finite values.
Results may differ from the reference program's by a relative error of at most 0.01.
Values may be sent and summed in bfloat16 or wider, within the bound.
No kernel may reach another device: no remote copies, remote signals or barrier semaphores. Data moves between devices by JAX's collectives and lax.ppermute only.
A program may use at most 64 MiB of HBM per device.

```python
import math
import jax
import jax.numpy as jnp
from jax import lax

K = 128
TB = 128
SUB = 256
TILES = 64
VERTS = 8192
N_ROW = 4
N_COL = 8


def draw_live_count(key, part):
    first_key, second_key = jax.random.split(jax.random.fold_in(key, 11))
    devices_all = N_ROW * N_COL
    reduced = TILES - jax.random.randint(first_key, (devices_all,), 0, 3 * TILES // 4 + 1)
    fullest = jax.random.randint(second_key, (), 0, devices_all)
    counts = jnp.where(jnp.arange(devices_all) == fullest, TILES, reduced)
    return counts.reshape(N_ROW, N_COL).astype(jnp.int32)


def place_ends(array, stream_key, smallest, high):
    index_at = [jax.random.randint(jax.random.fold_in(stream_key, axis), (), 0, length) for axis, length in enumerate(array.shape)]
    widest = array.shape.index(max(array.shape))
    beside = index_at[:widest] + [(index_at[widest] + 1) % array.shape[widest]] + index_at[widest + 1:]
    return array.at[tuple(index_at)].set(smallest).at[tuple(beside)].set(high)


def level_of(key, extent, cuts, low, largest):
    def one(axis_at, shards_of):
        heights = jax.random.uniform(jax.random.fold_in(jax.random.fold_in(key, 6), axis_at), (shards_of,), jnp.float32, low / len(cuts), largest / len(cuts))
        return jnp.repeat(jnp.exp(heights), extent[axis_at] // shards_of).reshape((-1,) + (1,) * (len(extent) - axis_at - 1))

    gain = one(*cuts[0])
    for cut in cuts[1:]:
        gain = gain * one(*cut)
    return gain


def bell_draw(own_key, dims, scale, reach, shards=(), held_as=jnp.bfloat16):
    values = jax.random.normal(own_key, dims, jnp.float32) * scale
    if len(shards) > 0:
        values = level_of(own_key, dims, shards, -0.22, 0.18) * values
    return jnp.clip(values, min=-reach, max=reach).astype(held_as)


def setup_inputs(seed: int = 0) -> dict:
    seeds = jax.random.split(jax.random.key(seed), 9)
    return {
        "start_block": bell_draw(seeds[0], (VERTS, K), 1.0, 6.0, ((0, 32),), jnp.float32),
        "vertex_scale": jnp.clip(jnp.exp(math.log(0.088388346) - 1.3862944 * jax.random.uniform(seeds[1], (VERTS,), jnp.float32) ** level_of(seeds[1], (VERTS,), ((0, 32),), -0.2, 0.2)), 0.022097087, 0.088388346),
        "adj_tiles": jnp.clip(1.0 * jax.random.uniform(seeds[2], (N_ROW, N_COL, TILES, TB, TB), jnp.float32) ** level_of(seeds[2], (N_ROW, N_COL, TILES, TB, TB), ((0, 4), (1, 8)), -0.2, 0.2), 0.0, 1.0).astype(jnp.bfloat16),
        "tile_row": place_ends(jax.random.randint(seeds[3], (N_ROW, N_COL, TILES), 0, N_ROW * SUB // TB), jax.random.fold_in(seeds[3], 1), 0, (N_ROW * SUB // TB) - 1).astype(jnp.int32),
        "tile_col": place_ends(jax.random.randint(seeds[4], (N_ROW, N_COL, TILES), 0, N_COL * SUB // TB), jax.random.fold_in(seeds[4], 1), 0, (N_COL * SUB // TB) - 1).astype(jnp.int32),
        "live_count": draw_live_count(jax.random.fold_in(seeds[8], 71), 0),
        "rotation_first": bell_draw(seeds[6], (2 * K, K), (2 * K) ** -0.5, 0.375, (), jnp.float32),
        "rotation_second": bell_draw(seeds[7], (3 * K, K), (3 * K) ** -0.5, 0.3125, (), jnp.float32),
    }


HIGH = lax.Precision.HIGHEST

def apply_operator(block, vertex_scale, adj_tiles, tile_row, tile_col, live_count):
    scaled = (vertex_scale[:, None] * block).astype(jnp.bfloat16)
    panels = scaled.reshape(N_ROW, N_COL * SUB // TB, TB, K)
    row_tiles = N_ROW * SUB // TB
    slot_ids = jnp.arange(TILES, dtype=jnp.int32)

    def device_partial(i, j):
        pieces = panels[i][tile_col[i, j]].astype(jnp.float32)
        tile_out = jnp.einsum('tab,tbk->tak', adj_tiles[i, j].astype(jnp.float32), pieces)
        tile_out = jnp.where((slot_ids < live_count[i, j])[:, None, None], tile_out, 0.0)
        partial_value = jax.ops.segment_sum(tile_out, tile_row[i, j], num_segments=row_tiles)
        partial_value = lax.optimization_barrier(partial_value.reshape(N_ROW, SUB, K).astype(jnp.bfloat16))
        return partial_value.astype(jnp.float32)

    def one_column(j):

        def add_row(i, running):
            return running + device_partial(i, j)
        return lax.fori_loop(0, N_ROW, add_row, jnp.zeros((N_ROW, SUB, K), jnp.float32))
    columns = lax.map(one_column, jnp.arange(N_COL, dtype=jnp.int32))
    summed = jnp.transpose(columns, (1, 0, 2, 3)).reshape(N_ROW * N_COL * SUB, K)
    return block - vertex_scale[:, None] * summed

def residual_block(block, image):
    gram = jnp.dot(block.T, image, precision=HIGH) / VERTS
    resid = image - jnp.dot(block, gram, precision=HIGH)
    colsq = lax.optimization_barrier(jnp.sum(resid * resid, axis=0))
    return resid * lax.rsqrt(colsq / VERTS + 1e-06)

def reference(start_block, vertex_scale, adj_tiles, tile_row, tile_col, live_count, rotation_first, rotation_second):

    def oper(block):
        return apply_operator(block, vertex_scale, adj_tiles, tile_row, tile_col, live_count)
    image0 = oper(start_block)
    search0 = residual_block(start_block, image0)
    simage0 = oper(search0)
    rot_x, rot_w = (rotation_first[:K], rotation_first[K:])
    block1 = jnp.dot(start_block, rot_x, precision=HIGH) + jnp.dot(search0, rot_w, precision=HIGH)
    image1 = jnp.dot(image0, rot_x, precision=HIGH) + jnp.dot(simage0, rot_w, precision=HIGH)
    prev1 = jnp.dot(search0, rot_w, precision=HIGH)
    pimage1 = jnp.dot(simage0, rot_w, precision=HIGH)
    search1 = residual_block(block1, image1)
    simage1 = oper(search1)
    qx, qw, qp = (rotation_second[:K], rotation_second[K:2 * K], rotation_second[2 * K:])
    final_block = jnp.dot(block1, qx, precision=HIGH) + jnp.dot(search1, qw, precision=HIGH) + jnp.dot(prev1, qp, precision=HIGH)
    final_image = jnp.dot(image1, qx, precision=HIGH) + jnp.dot(simage1, qw, precision=HIGH) + jnp.dot(pimage1, qp, precision=HIGH)
    return (final_block, final_image)
```

```python
import functools

import jax
import jax.numpy as jnp
from jax import lax
from jax.experimental import pallas as pl
from jax.experimental.pallas import tpu as pltpu
from jax.sharding import PartitionSpec as P

HIGH = lax.Precision.HIGHEST
VMEM_BYTES = 40 * 1024 * 1024


def swap(array, axis, mask):
    size = lax.axis_size(axis)
    return lax.ppermute(array, axis, [(k, k ^ mask) for k in range(size)])


def vmem(count):
    return [pl.BlockSpec(memory_space=pltpu.VMEM)] * count


def smem(count):
    return [pl.BlockSpec(memory_space=pltpu.SMEM)] * count


def dot(left, right, contract=((1,), (0,))):
    return lax.dot_general(
        left, right, (contract, ((), ())), precision=HIGH, preferred_element_type=jnp.float32
    )


def tiles_kernel(n_col, n_row, unroll, cols_ref, rows_ref, tiles_ref, *refs):
    pieces, outs = refs[:n_col], refs[n_col : n_col + n_row]
    panel, total = refs[n_col + n_row :]
    sub = pieces[0].shape[0]
    slots, side = tiles_ref.shape[0], tiles_ref.shape[1]
    for m, piece in enumerate(pieces):
        panel[m * sub : (m + 1) * sub] = piece[...]
    total[...] = jnp.zeros_like(total)

    def step(group, carry):
        products = []
        for u in range(unroll):
            slot = group * unroll + u
            column = pl.multiple_of(cols_ref[slot] * side, side)
            products.append(
                jnp.dot(
                    tiles_ref[slot],
                    panel[pl.ds(column, side), :],
                    preferred_element_type=jnp.float32,
                )
            )
        for u in range(unroll):
            row = pl.multiple_of(rows_ref[group * unroll + u] * side, side)
            total[pl.ds(row, side), :] += products[u]
        return carry

    lax.fori_loop(0, slots // unroll, step, 0)
    outs[0][...] = total[:sub]
    for k in range(1, n_row):
        outs[k][...] = total[k * sub : (k + 1) * sub].astype(outs[k].dtype)


def tile_products(cols, rows, tiles, pieces, n_row):
    n_col = len(pieces)
    sub, width = pieces[0].shape
    slots, side = tiles.shape[0], tiles.shape[1]
    unroll = 4 if slots % 4 == 0 else 1
    return pl.pallas_call(
        functools.partial(tiles_kernel, n_col, n_row, unroll),
        out_shape=[
            jax.ShapeDtypeStruct((sub, width), jnp.float32 if k == 0 else jnp.bfloat16)
            for k in range(n_row)
        ],
        in_specs=smem(2) + vmem(1 + n_col),
        out_specs=vmem(n_row),
        scratch_shapes=[
            pltpu.VMEM((n_col * sub, width), jnp.bfloat16),
            pltpu.VMEM((n_row * sub + side, width), jnp.float32),
        ],
        compiler_params=pltpu.CompilerParams(vmem_limit_bytes=VMEM_BYTES),
        cost_estimate=pl.CostEstimate(
            flops=2 * slots * side * side * width,
            bytes_accessed=2 * slots * side * side,
            transcendentals=0,
        ),
        name="tile_products",
    )(cols, rows, tiles, *pieces)


def gram_kernel(n_col, index_ref, x_ref, z1_ref, z2_ref, near_ref, far_ref, whole):
    x, z1, z2 = x_ref[...], z1_ref[...], z2_ref[...]
    contract = ((0,), (0,))
    for at, (left, right) in enumerate(
        ((x, x), (x, z1), (z1, z1), (x, z2), (z1, z2), (z2, z2))
    ):
        whole[at] = dot(left, right, contract)
    rows = whole.shape[1] // n_col
    for m in range(n_col):
        out = far_ref if m % 2 else near_ref
        start = pl.multiple_of((index_ref[0] ^ m) * rows, rows)
        for at in range(whole.shape[0]):
            out[m // 2, at * rows : (at + 1) * rows] = whole[at, pl.ds(start, rows), :]


def grams(index, x, z1, z2, n_col):
    width = x.shape[1]
    cut = jax.ShapeDtypeStruct((n_col // 2, 6 * (width // n_col), width), jnp.float32)
    return pl.pallas_call(
        functools.partial(gram_kernel, n_col),
        out_shape=[cut, cut],
        in_specs=smem(1) + vmem(3),
        out_specs=vmem(2),
        scratch_shapes=[pltpu.VMEM((6, width, width), jnp.float32)],
        compiler_params=pltpu.CompilerParams(vmem_limit_bytes=VMEM_BYTES),
        name="grams",
    )(index, x, z1, z2)


def finish_kernel(
    n_col,
    verts_all,
    index_ref,
    x_ref,
    z1_ref,
    z2_ref,
    z3_ref,
    first_ref,
    second_ref,
    near_ref,
    far_ref,
    block_ref,
    image_ref,
    whole,
):
    width = x_ref.shape[1]
    rows = width // n_col
    for m in range(n_col):
        piece = far_ref if m % 2 else near_ref
        start = pl.multiple_of((index_ref[0] ^ m) * rows, rows)
        for at in range(whole.shape[0]):
            whole[at, pl.ds(start, rows), :] = piece[m // 2, at * rows : (at + 1) * rows]
    n00, n01, n11, n02, n12, n22 = (whole[at] for at in range(6))
    n10, n21 = n01.T, n12.T
    eye = (
        lax.broadcasted_iota(jnp.int32, (width, width), 0)
        == lax.broadcasted_iota(jnp.int32, (width, width), 1)
    ).astype(jnp.float32)
    scale = 1.0 / verts_all

    def inverse_norm(colsq):
        row = lax.rsqrt(jnp.maximum(colsq, 0.0) * scale + 1e-06)
        return jnp.sum(eye * row, axis=1, keepdims=True)

    def column_sum(array):
        return jnp.sum(array, axis=0, keepdims=True)

    keep0 = eye - (n00 - n01) * scale
    colsq0 = column_sum(keep0 * (dot(n00, keep0) - 2.0 * n01) + eye * n11)
    q = inverse_norm(colsq0) * first_ref[width:]
    p = first_ref[:width] + dot(keep0, q)
    coeff = jnp.concatenate([p, -q], axis=0)
    blocks = jnp.concatenate(
        [
            jnp.concatenate([n00, n01], axis=1),
            jnp.concatenate([n10, n11], axis=1),
            jnp.concatenate([n01, n02], axis=1),
            jnp.concatenate([n11, n12], axis=1),
            jnp.concatenate([n11, n12], axis=1),
            jnp.concatenate([n21, n22], axis=1),
        ],
        axis=0,
    )
    applied = dot(blocks, coeff)
    pair = jnp.concatenate(
        [applied[: 2 * width], applied[2 * width : 4 * width]], axis=1
    )
    both = dot(coeff, pair, ((0,), (0,)))
    s, t = both[:, :width], both[:, width:]
    u = column_sum(coeff * applied[4 * width :])
    keep1 = eye - (s - t) * scale
    colsq1 = column_sum(keep1 * (dot(s, keep1) - 2.0 * t)) + u
    v = inverse_norm(colsq1) * second_ref[width : 2 * width]
    e = second_ref[:width] + dot(keep1, v)
    f = dot(q, second_ref[2 * width :])
    mixed = dot(jnp.concatenate([p, q], axis=0), jnp.concatenate([e, v], axis=1))
    a0 = mixed[:width, :width] + dot(keep0, f)
    a1 = -(mixed[width:, :width] + mixed[:width, width:] + f)
    a2 = mixed[width:, width:]
    stacked = jnp.concatenate([a0, a1, a2], axis=0)
    z1, z2 = z1_ref[...], z2_ref[...]
    block = dot(jnp.concatenate([x_ref[...], z1, z2], axis=1), stacked)
    block_ref[...] = block
    image_ref[...] = block - dot(jnp.concatenate([z1, z2, z3_ref[...]], axis=1), stacked)


def finish(index, x, z1, z2, z3, first, second, near, far, n_col, verts_all):
    out = jax.ShapeDtypeStruct(x.shape, jnp.float32)
    width = x.shape[1]
    return pl.pallas_call(
        functools.partial(finish_kernel, n_col, verts_all),
        out_shape=[out, out],
        in_specs=smem(1) + vmem(8),
        out_specs=vmem(2),
        scratch_shapes=[pltpu.VMEM((6, width, width), jnp.float32)],
        compiler_params=pltpu.CompilerParams(vmem_limit_bytes=VMEM_BYTES),
        name="finish",
    )(index, x, z1, z2, z3, first, second, near, far)


def local(
    start_block,
    vertex_scale,
    adj_tiles,
    tile_row,
    tile_col,
    live_count,
    rotation_first,
    rotation_second,
):
    n_row, n_col = lax.axis_size("row"), lax.axis_size("col")
    row_at, col_at = lax.axis_index("row"), lax.axis_index("col")
    sub = start_block.shape[0]
    verts_all = sub * n_row * n_col
    tiles = adj_tiles[0, 0]
    halves = sub // tiles.shape[1]
    slots = jnp.arange(tiles.shape[0], dtype=jnp.int32)
    cols = ((tile_col[0, 0] // halves) ^ col_at) * halves + tile_col[0, 0] % halves
    rows = ((tile_row[0, 0] // halves) ^ row_at) * halves + tile_row[0, 0] % halves
    rows = jnp.where(slots < live_count[0, 0], rows, n_row * halves)
    index = col_at.reshape(1)
    scale = vertex_scale[:, None]

    def adjacency(block):
        own = (scale * block).astype(jnp.bfloat16)
        near = [own] + [swap(own, "col", m) for m in range(2, n_col, 2)]
        far = [swap(piece, "col", 1) for piece in near]
        pieces = [piece for pair in zip(near, far) for piece in pair]
        parts = tile_products(cols, rows, tiles, pieces, n_row)
        summed = parts[0]
        for k in range(1, n_row):
            summed = summed + swap(parts[k], "row", k).astype(jnp.float32)
        return scale * summed

    z1 = adjacency(start_block)
    z2 = adjacency(z1)
    near, far = grams(index, start_block, z1, z2, n_col)
    near = near + swap(far, "col", 1)
    mine = near[0]
    for q in range(1, n_col // 2):
        mine = mine + swap(near[q], "col", 2 * q)
    whole = mine
    for k in range(1, n_row):
        whole = whole + swap(mine, "row", k)
    near = jnp.stack([whole] + [swap(whole, "col", m) for m in range(2, n_col, 2)])
    far = swap(near, "col", 1)
    z3 = adjacency(z2)
    return tuple(
        finish(
            index,
            start_block,
            z1,
            z2,
            z3,
            rotation_first,
            rotation_second,
            near,
            far,
            n_col,
            verts_all,
        )
    )


def solution(mesh):
    placed = (
        P(("row", "col"), None),
        P(("row", "col")),
        P("row", "col", None, None, None),
        P("row", "col", None),
        P("row", "col", None),
        P("row", "col"),
        P(),
        P(),
    )
    return jax.shard_map(
        local,
        mesh=mesh,
        in_specs=placed,
        out_specs=(P(("row", "col"), None), P(("row", "col"), None)),
        check_vma=False,
    )
```

```python
import functools

import jax
import jax.numpy as jnp
from jax import lax
from jax.experimental import pallas as pl
from jax.experimental.pallas import tpu as pltpu
from jax.sharding import PartitionSpec as P

HIGH = lax.Precision.HIGHEST
VMEM_BYTES = 2 * 1024 * 1024
DENSE_BYTES = 8 * 1024 * 1024


def swap(array, axis, mask):
    size = lax.axis_size(axis)
    return lax.ppermute(array, axis, [(k, k ^ mask) for k in range(size)])


def vmem(count):
    return [pl.BlockSpec(memory_space=pltpu.VMEM)] * count


def smem(count):
    return [pl.BlockSpec(memory_space=pltpu.SMEM)] * count


def dot(left, right, contract=((1,), (0,))):
    return lax.dot_general(
        left, right, (contract, ((), ())), precision=HIGH, preferred_element_type=jnp.float32
    )


def tiles_kernel(n_col, n_row, unroll, cols_ref, rows_ref, tiles_ref, *refs):
    pieces, outs = refs[:n_col], refs[n_col : n_col + n_row]
    panel, total = refs[n_col + n_row :]
    sub = pieces[0].shape[0]
    slots, side = tiles_ref.shape[0], tiles_ref.shape[1]
    for m, piece in enumerate(pieces):
        panel[m * sub : (m + 1) * sub] = piece[...]
    total[...] = jnp.zeros_like(total)

    def step(group, carry):
        products = []
        for u in range(unroll):
            slot = group * unroll + u
            column = pl.multiple_of(cols_ref[slot] * side, side)
            products.append(
                jnp.dot(
                    tiles_ref[slot],
                    panel[pl.ds(column, side), :],
                    preferred_element_type=jnp.float32,
                )
            )
        for u in range(unroll):
            row = pl.multiple_of(rows_ref[group * unroll + u] * side, side)
            total[pl.ds(row, side), :] += products[u]
        return carry

    lax.fori_loop(0, slots // unroll, step, 0)
    outs[0][...] = total[:sub]
    for k in range(1, n_row):
        outs[k][...] = total[k * sub : (k + 1) * sub].astype(outs[k].dtype)


def tile_products(cols, rows, tiles, pieces, n_row):
    n_col = len(pieces)
    sub, width = pieces[0].shape
    slots, side = tiles.shape[0], tiles.shape[1]
    unroll = 4 if slots % 4 == 0 else 1
    return pl.pallas_call(
        functools.partial(tiles_kernel, n_col, n_row, unroll),
        out_shape=[
            jax.ShapeDtypeStruct((sub, width), jnp.float32 if k == 0 else jnp.bfloat16)
            for k in range(n_row)
        ],
        in_specs=smem(2) + vmem(1 + n_col),
        out_specs=vmem(n_row),
        scratch_shapes=[
            pltpu.VMEM((n_col * sub, width), jnp.bfloat16),
            pltpu.VMEM((n_row * sub + side, width), jnp.float32),
        ],
        compiler_params=pltpu.CompilerParams(vmem_limit_bytes=8 * VMEM_BYTES),
        cost_estimate=pl.CostEstimate(
            flops=2 * slots * side * side * width,
            bytes_accessed=2 * slots * side * side,
            transcendentals=0,
        ),
        name="tile_products",
    )(cols, rows, tiles, *pieces)


def place_kernel(count_ref, cols_ref, rows_ref, tiles_ref, dense_ref):
    side = tiles_ref.shape[1]
    dense_ref[...] = jnp.zeros_like(dense_ref)

    def step(slot, carry):
        row = pl.multiple_of(rows_ref[slot] * side, side)
        column = pl.multiple_of(cols_ref[slot] * side, side)
        at = (pl.ds(row, side), pl.ds(column, side))
        total = dense_ref[at].astype(jnp.float32) + tiles_ref[slot].astype(jnp.float32)
        dense_ref[at] = total.astype(dense_ref.dtype)
        return carry

    lax.fori_loop(0, jnp.minimum(count_ref[0], tiles_ref.shape[0]), step, 0)


def place_tiles(count, cols, rows, tiles, height, width):
    return pl.pallas_call(
        place_kernel,
        out_shape=jax.ShapeDtypeStruct((height, width), jnp.bfloat16),
        in_specs=smem(3) + vmem(1),
        out_specs=vmem(1)[0],
        compiler_params=pltpu.CompilerParams(vmem_limit_bytes=VMEM_BYTES),
        cost_estimate=pl.CostEstimate(
            flops=0, bytes_accessed=4 * height * width, transcendentals=0
        ),
        name="place_tiles",
    )(count, cols, rows, tiles)


def dense_kernel(n_col, n_row, dense_ref, *refs):
    pieces, outs, panel = refs[:n_col], refs[n_col : n_col + n_row], refs[-1]
    sub = pieces[0].shape[0]
    for m, piece in enumerate(pieces):
        panel[m * sub : (m + 1) * sub] = piece[...]
    for k in range(n_row):
        part = jnp.dot(
            dense_ref[k * sub : (k + 1) * sub], panel[...], preferred_element_type=jnp.float32
        )
        outs[k][...] = part.astype(outs[k].dtype)


def dense_products(dense, pieces, n_row):
    n_col = len(pieces)
    sub, width = pieces[0].shape
    return pl.pallas_call(
        functools.partial(dense_kernel, n_col, n_row),
        out_shape=[
            jax.ShapeDtypeStruct((sub, width), jnp.float32 if k == 0 else jnp.bfloat16)
            for k in range(n_row)
        ],
        in_specs=vmem(1 + n_col),
        out_specs=vmem(n_row),
        scratch_shapes=[pltpu.VMEM((n_col * sub, width), jnp.bfloat16)],
        compiler_params=pltpu.CompilerParams(vmem_limit_bytes=VMEM_BYTES),
        cost_estimate=pl.CostEstimate(
            flops=2 * dense.size * width, bytes_accessed=2 * dense.size, transcendentals=0
        ),
        name="dense_products",
    )(dense, *pieces)


def gram_kernel(pieces, index_ref, x_ref, z1_ref, z2_ref, near_ref, far_ref, whole):
    x, z1, z2 = x_ref[...], z1_ref[...], z2_ref[...]
    contract = ((0,), (0,))
    for at, (left, right) in enumerate(
        ((x, x), (x, z1), (z1, z1), (x, z2), (z1, z2), (z2, z2))
    ):
        whole[at] = dot(left, right, contract)
    rows = whole.shape[1] // pieces
    for m in range(pieces):
        out = far_ref if m % 2 else near_ref
        start = pl.multiple_of((index_ref[0] ^ m) * rows, rows)
        for at in range(whole.shape[0]):
            out[m // 2, at * rows : (at + 1) * rows] = whole[at, pl.ds(start, rows), :]


def grams(index, x, z1, z2, pieces):
    width = x.shape[1]
    cut = jax.ShapeDtypeStruct((pieces // 2, 6 * (width // pieces), width), jnp.float32)
    return pl.pallas_call(
        functools.partial(gram_kernel, pieces),
        out_shape=[cut, cut],
        in_specs=smem(1) + vmem(3),
        out_specs=vmem(2),
        scratch_shapes=[pltpu.VMEM((6, width, width), jnp.float32)],
        compiler_params=pltpu.CompilerParams(vmem_limit_bytes=VMEM_BYTES),
        name="grams",
    )(index, x, z1, z2)


def finish_kernel(
    pieces,
    verts_all,
    index_ref,
    x_ref,
    z1_ref,
    z2_ref,
    z3_ref,
    first_ref,
    second_ref,
    near_ref,
    far_ref,
    block_ref,
    image_ref,
    whole,
):
    width = x_ref.shape[1]
    rows = width // pieces
    for m in range(pieces):
        piece = far_ref if m % 2 else near_ref
        start = pl.multiple_of((index_ref[0] ^ m) * rows, rows)
        for at in range(whole.shape[0]):
            whole[at, pl.ds(start, rows), :] = piece[m // 2, at * rows : (at + 1) * rows]
    n00, n01, n11, n02, n12, n22 = (whole[at] for at in range(6))
    n10, n21 = n01.T, n12.T
    eye = (
        lax.broadcasted_iota(jnp.int32, (width, width), 0)
        == lax.broadcasted_iota(jnp.int32, (width, width), 1)
    ).astype(jnp.float32)
    scale = 1.0 / verts_all

    def inverse_norm(colsq):
        row = lax.rsqrt(jnp.maximum(colsq, 0.0) * scale + 1e-06)
        return jnp.sum(eye * row, axis=1, keepdims=True)

    def column_sum(array):
        return jnp.sum(array, axis=0, keepdims=True)

    keep0 = eye - (n00 - n01) * scale
    colsq0 = column_sum(keep0 * (dot(n00, keep0) - 2.0 * n01) + eye * n11)
    q = inverse_norm(colsq0) * first_ref[width:]
    p = first_ref[:width] + dot(keep0, q)
    coeff = jnp.concatenate([p, -q], axis=0)
    blocks = jnp.concatenate(
        [
            jnp.concatenate([n00, n01], axis=1),
            jnp.concatenate([n10, n11], axis=1),
            jnp.concatenate([n01, n02], axis=1),
            jnp.concatenate([n11, n12], axis=1),
            jnp.concatenate([n11, n12], axis=1),
            jnp.concatenate([n21, n22], axis=1),
        ],
        axis=0,
    )
    applied = dot(blocks, coeff)
    pair = jnp.concatenate(
        [applied[: 2 * width], applied[2 * width : 4 * width]], axis=1
    )
    both = dot(coeff, pair, ((0,), (0,)))
    s, t = both[:, :width], both[:, width:]
    u = column_sum(coeff * applied[4 * width :])
    keep1 = eye - (s - t) * scale
    colsq1 = column_sum(keep1 * (dot(s, keep1) - 2.0 * t)) + u
    v = inverse_norm(colsq1) * second_ref[width : 2 * width]
    e = second_ref[:width] + dot(keep1, v)
    f = dot(q, second_ref[2 * width :])
    mixed = dot(jnp.concatenate([p, q], axis=0), jnp.concatenate([e, v], axis=1))
    a0 = mixed[:width, :width] + dot(keep0, f)
    a1 = -(mixed[width:, :width] + mixed[:width, width:] + f)
    a2 = mixed[width:, width:]
    none = jnp.zeros_like(a0)
    spread = jnp.concatenate(
        [
            jnp.concatenate([a0, none], axis=1),
            jnp.concatenate([a1, a0], axis=1),
            jnp.concatenate([a2, a1], axis=1),
            jnp.concatenate([none, a2], axis=1),
        ],
        axis=0,
    )
    basis = jnp.concatenate([x_ref[...], z1_ref[...], z2_ref[...], z3_ref[...]], axis=1)
    result = dot(basis, spread)
    block_ref[...] = result[:, :width]
    image_ref[...] = result[:, :width] - result[:, width:]


def finish(index, x, z1, z2, z3, first, second, near, far, pieces, verts_all):
    out = jax.ShapeDtypeStruct(x.shape, jnp.float32)
    width = x.shape[1]
    return pl.pallas_call(
        functools.partial(finish_kernel, pieces, verts_all),
        out_shape=[out, out],
        in_specs=smem(1) + vmem(8),
        out_specs=vmem(2),
        scratch_shapes=[pltpu.VMEM((6, width, width), jnp.float32)],
        compiler_params=pltpu.CompilerParams(vmem_limit_bytes=4 * VMEM_BYTES),
        name="finish",
    )(index, x, z1, z2, z3, first, second, near, far)


def local(
    start_block,
    vertex_scale,
    adj_tiles,
    tile_row,
    tile_col,
    live_count,
    rotation_first,
    rotation_second,
):
    n_row, n_col = lax.axis_size("row"), lax.axis_size("col")
    row_at, col_at = lax.axis_index("row"), lax.axis_index("col")
    sub = start_block.shape[0]
    verts_all = sub * n_row * n_col
    tiles = adj_tiles[0, 0]
    halves = sub // tiles.shape[1]
    slots = jnp.arange(tiles.shape[0], dtype=jnp.int32)
    cols = ((tile_col[0, 0] // halves) ^ col_at) * halves + tile_col[0, 0] % halves
    rows = ((tile_row[0, 0] // halves) ^ row_at) * halves + tile_row[0, 0] % halves
    dense = None
    if 2 * n_row * n_col * sub * sub <= DENSE_BYTES:
        dense = place_tiles(live_count[0], cols, rows, tiles, n_row * sub, n_col * sub)
    else:
        rows = jnp.where(slots < live_count[0, 0], rows, n_row * halves)
    width = start_block.shape[1]
    scale = vertex_scale[:, None]

    def gather(block, dense=None):
        own = (scale * block).astype(jnp.bfloat16)
        near = [own] + [swap(own, "col", m) for m in range(2, n_col, 2)]
        if dense is not None:
            own, dense = lax.optimization_barrier((own, dense))
        return near, [swap(piece, "col", 1) for piece in [own] + near[1:]]

    def multiply(near, far):
        pieces = [piece for pair in zip(near, far) for piece in pair]
        if dense is None:
            return tile_products(cols, rows, tiles, pieces, n_row)
        return dense_products(dense, pieces, n_row)

    def send(parts):
        return [parts[0]] + [swap(parts[k], "row", k) for k in range(1, n_row)]

    def collect(parts):
        summed = parts[0]
        for part in parts[1:]:
            summed = summed + part.astype(jnp.float32)
        return scale * summed

    inner = [("col", m) for m in range(2, n_col, 2)]
    outer = [("row", k) for k in range(1, n_row)]
    place = 2 * row_at + col_at % 2
    if (width // (2 * n_row)) % 8 != 0:
        inner, outer, place = outer, inner, col_at
    index = place.reshape(1)

    def cut_grams(x, z1, z2):
        near, far = grams(index, x, z1, z2, 2 * (len(outer) + 1))
        near = near + swap(far, "col", 1)
        return near[0], [swap(near[q + 1], *hop) for q, hop in enumerate(outer)]

    def add(mine, arrived):
        for piece in arrived:
            mine = mine + piece
        return mine

    z1 = collect(send(multiply(*gather(start_block, dense))))
    z2 = collect(send(multiply(*gather(z1))))
    near, far = gather(z2)
    mine, arrived = cut_grams(start_block, z1, z2)
    mine = add(mine, arrived)
    arrived = [swap(mine, *hop) for hop in inner]
    parts, arrived = lax.optimization_barrier((multiply(near, far), arrived))
    whole = add(mine, arrived)
    gram_near = jnp.stack([whole] + [swap(whole, *hop) for hop in outer])
    gram_far = swap(gram_near, "col", 1)
    z3 = collect(send(parts))
    return tuple(
        finish(
            index,
            start_block,
            z1,
            z2,
            z3,
            rotation_first,
            rotation_second,
            gram_near,
            gram_far,
            2 * gram_near.shape[0],
            verts_all,
        )
    )


def solution(mesh):
    placed = (
        P(("row", "col"), None),
        P(("row", "col")),
        P("row", "col", None, None, None),
        P("row", "col", None),
        P("row", "col", None),
        P("row", "col"),
        P(),
        P(),
    )
    return jax.shard_map(
        local,
        mesh=mesh,
        in_specs=placed,
        out_specs=(P(("row", "col"), None), P(("row", "col"), None)),
        check_vma=False,
    )
```

```python
import functools

import jax
import jax.numpy as jnp
from jax import lax
from jax.experimental import pallas as pl
from jax.experimental.pallas import tpu as pltpu
from jax.sharding import PartitionSpec as P

HIGH = lax.Precision.HIGHEST
VMEM_BYTES = 2 * 1024 * 1024
DENSE_BYTES = 8 * 1024 * 1024


def swap(array, axis, mask):
    size = lax.axis_size(axis)
    return lax.ppermute(array, axis, [(k, k ^ mask) for k in range(size)])


def vmem(count):
    return [pl.BlockSpec(memory_space=pltpu.VMEM)] * count


def smem(count):
    return [pl.BlockSpec(memory_space=pltpu.SMEM)] * count


def dot(left, right, contract=((1,), (0,))):
    return lax.dot_general(
        left, right, (contract, ((), ())), precision=HIGH, preferred_element_type=jnp.float32
    )


def dot_short(left, right):
    left_high, right_high = left.astype(jnp.bfloat16), right.astype(jnp.bfloat16)
    left_low = (left - left_high.astype(jnp.float32)).astype(jnp.bfloat16)
    right_low = (right - right_high.astype(jnp.float32)).astype(jnp.bfloat16)
    return jnp.dot(
        jnp.concatenate([left_low, left_high, left_high], axis=1),
        jnp.concatenate([right_high, right_low, right_high], axis=0),
        preferred_element_type=jnp.float32,
    )


def tiles_kernel(n_col, n_row, unroll, cols_ref, rows_ref, tiles_ref, *refs):
    pieces, outs = refs[:n_col], refs[n_col : n_col + n_row]
    panel, total = refs[n_col + n_row :]
    sub = pieces[0].shape[0]
    slots, side = tiles_ref.shape[0], tiles_ref.shape[1]
    for m, piece in enumerate(pieces):
        panel[m * sub : (m + 1) * sub] = piece[...]
    total[...] = jnp.zeros_like(total)

    def step(group, carry):
        products = []
        for u in range(unroll):
            slot = group * unroll + u
            column = pl.multiple_of(cols_ref[slot] * side, side)
            products.append(
                jnp.dot(
                    tiles_ref[slot],
                    panel[pl.ds(column, side), :],
                    preferred_element_type=jnp.float32,
                )
            )
        for u in range(unroll):
            row = pl.multiple_of(rows_ref[group * unroll + u] * side, side)
            total[pl.ds(row, side), :] += products[u]
        return carry

    lax.fori_loop(0, slots // unroll, step, 0)
    outs[0][...] = total[:sub]
    for k in range(1, n_row):
        outs[k][...] = total[k * sub : (k + 1) * sub].astype(outs[k].dtype)


def tile_products(cols, rows, tiles, pieces, n_row):
    n_col = len(pieces)
    sub, width = pieces[0].shape
    slots, side = tiles.shape[0], tiles.shape[1]
    unroll = 4 if slots % 4 == 0 else 1
    return pl.pallas_call(
        functools.partial(tiles_kernel, n_col, n_row, unroll),
        out_shape=[
            jax.ShapeDtypeStruct((sub, width), jnp.float32 if k == 0 else jnp.bfloat16)
            for k in range(n_row)
        ],
        in_specs=smem(2) + vmem(1 + n_col),
        out_specs=vmem(n_row),
        scratch_shapes=[
            pltpu.VMEM((n_col * sub, width), jnp.bfloat16),
            pltpu.VMEM((n_row * sub + side, width), jnp.float32),
        ],
        compiler_params=pltpu.CompilerParams(vmem_limit_bytes=8 * VMEM_BYTES),
        cost_estimate=pl.CostEstimate(
            flops=2 * slots * side * side * width,
            bytes_accessed=2 * slots * side * side,
            transcendentals=0,
        ),
        name="tile_products",
    )(cols, rows, tiles, *pieces)


def place_kernel(count_ref, cols_ref, rows_ref, tiles_ref, dense_ref):
    side = tiles_ref.shape[1]
    dense_ref[...] = jnp.zeros_like(dense_ref)

    def step(slot, carry):
        row = pl.multiple_of(rows_ref[slot] * side, side)
        column = pl.multiple_of(cols_ref[slot] * side, side)
        at = (pl.ds(row, side), pl.ds(column, side))
        total = dense_ref[at].astype(jnp.float32) + tiles_ref[slot].astype(jnp.float32)
        dense_ref[at] = total.astype(dense_ref.dtype)
        return carry

    lax.fori_loop(0, jnp.minimum(count_ref[0], tiles_ref.shape[0]), step, 0)


def place_tiles(count, cols, rows, tiles, height, width):
    return pl.pallas_call(
        place_kernel,
        out_shape=jax.ShapeDtypeStruct((height, width), jnp.bfloat16),
        in_specs=smem(3) + vmem(1),
        out_specs=vmem(1)[0],
        compiler_params=pltpu.CompilerParams(vmem_limit_bytes=VMEM_BYTES),
        cost_estimate=pl.CostEstimate(
            flops=0, bytes_accessed=4 * height * width, transcendentals=0
        ),
        name="place_tiles",
    )(count, cols, rows, tiles)


def dense_kernel(n_col, n_row, dense_ref, *refs):
    pieces, outs, panel = refs[:n_col], refs[n_col : n_col + n_row], refs[-1]
    sub = pieces[0].shape[0]
    for m, piece in enumerate(pieces):
        panel[m * sub : (m + 1) * sub] = piece[...]
    for k in range(n_row):
        part = jnp.dot(
            dense_ref[k * sub : (k + 1) * sub], panel[...], preferred_element_type=jnp.float32
        )
        outs[k][...] = part.astype(outs[k].dtype)


def dense_products(dense, pieces, n_row):
    n_col = len(pieces)
    sub, width = pieces[0].shape
    return pl.pallas_call(
        functools.partial(dense_kernel, n_col, n_row),
        out_shape=[
            jax.ShapeDtypeStruct((sub, width), jnp.float32 if k == 0 else jnp.bfloat16)
            for k in range(n_row)
        ],
        in_specs=vmem(1 + n_col),
        out_specs=vmem(n_row),
        scratch_shapes=[pltpu.VMEM((n_col * sub, width), jnp.bfloat16)],
        compiler_params=pltpu.CompilerParams(vmem_limit_bytes=VMEM_BYTES),
        cost_estimate=pl.CostEstimate(
            flops=2 * dense.size * width, bytes_accessed=2 * dense.size, transcendentals=0
        ),
        name="dense_products",
    )(dense, *pieces)


def indices(width):
    return (
        lax.broadcasted_iota(jnp.int32, (width, width), 0),
        lax.broadcasted_iota(jnp.int32, (width, width), 1),
    )


def column_sum(array):
    return jnp.sum(array, axis=0, keepdims=True)


def gram_kernel(pieces, index_ref, x_ref, z1_ref, z2_ref, near_ref, far_ref, whole):
    x, z1, z2 = x_ref[...], z1_ref[...], z2_ref[...]
    width = x.shape[1]
    row, col = indices(width)
    eye = (row == col).astype(jnp.float32)
    contract = ((0,), (0,))
    n00 = dot(x, x, contract) - x.shape[0] * eye
    n11 = dot(z1, z1, contract)
    n22 = dot(z2, z2, contract)
    diagonal = column_sum(eye * n11)
    last = jnp.where((row == width - 2) & (col == 0), n11[width - 1 :, width - 1 :], 0.0)
    whole[0] = jnp.where(row <= col, n00, n11)
    whole[1] = jnp.where(row <= col, n22, jnp.where(row == width - 1, diagonal, last))
    whole[2] = dot(x, z1, contract)
    whole[3] = dot(x, z2, contract)
    whole[4] = dot(z1, z2, contract)
    rows = width // pieces
    for m in range(pieces):
        out = far_ref if m % 2 else near_ref
        start = pl.multiple_of((index_ref[0] ^ m) * rows, rows)
        for at in range(whole.shape[0]):
            out[m // 2, at * rows : (at + 1) * rows] = whole[at, pl.ds(start, rows), :]


def grams(index, x, z1, z2, pieces):
    width = x.shape[1]
    cut = jax.ShapeDtypeStruct((pieces // 2, 5 * (width // pieces), width), jnp.float32)
    return pl.pallas_call(
        functools.partial(gram_kernel, pieces),
        out_shape=[cut, cut],
        in_specs=smem(1) + vmem(3),
        out_specs=vmem(2),
        scratch_shapes=[pltpu.VMEM((5, width, width), jnp.float32)],
        compiler_params=pltpu.CompilerParams(vmem_limit_bytes=4 * VMEM_BYTES),
        name="grams",
    )(index, x, z1, z2)


def finish_kernel(
    pieces,
    verts_all,
    index_ref,
    x_ref,
    z1_ref,
    z2_ref,
    z3_ref,
    first_ref,
    second_ref,
    near_ref,
    far_ref,
    block_ref,
    image_ref,
    whole,
):
    width = x_ref.shape[1]
    rows = width // pieces
    for m in range(pieces):
        piece = far_ref if m % 2 else near_ref
        start = pl.multiple_of((index_ref[0] ^ m) * rows, rows)
        for at in range(whole.shape[0]):
            whole[at, pl.ds(start, rows), :] = piece[m // 2, at * rows : (at + 1) * rows]
    row, col = indices(width)
    eye = (row == col).astype(jnp.float32)
    first, third, n01, n02, n12 = (whole[at] for at in range(5))
    first_t = first.T
    diagonal = jnp.where(
        col[:1] == width - 1, third[width - 2 : width - 1, :1], third[width - 1 :, :]
    )
    excess = jnp.where(row <= col, first, first_t)
    n00 = excess + verts_all * eye
    n11 = jnp.where(row > col, first, jnp.where(row < col, first_t, diagonal))
    n22 = jnp.where(row <= col, third, third.T)
    n10, n21 = n01.T, n12.T
    scale = 1.0 / verts_all

    def inverse_norm(colsq):
        norm = lax.rsqrt(jnp.maximum(colsq, 0.0) * scale + 1e-06)
        return jnp.sum(eye * norm, axis=1, keepdims=True)

    keep0 = (n01 - excess) * scale
    colsq0 = column_sum(keep0 * (dot(n00, keep0) - 2.0 * n01) + eye * n11)
    q = inverse_norm(colsq0) * first_ref[width:]
    p = first_ref[:width] + dot(keep0, q)
    coeff = jnp.concatenate([p, -q], axis=0)
    blocks = jnp.concatenate(
        [
            jnp.concatenate([n00, n01], axis=1),
            jnp.concatenate([n10, n11], axis=1),
            jnp.concatenate([n01, n02], axis=1),
            jnp.concatenate([n11, n12], axis=1),
            jnp.concatenate([n21, n22], axis=1),
        ],
        axis=0,
    )
    applied = dot(blocks, coeff)
    pair = jnp.concatenate(
        [applied[: 2 * width], applied[2 * width : 4 * width]], axis=1
    )
    both = dot(coeff, pair, ((0,), (0,)))
    s, t = both[:, :width], both[:, width:]
    u = column_sum(coeff * applied[3 * width :])
    keep1 = eye - (s - t) * scale
    colsq1 = column_sum(keep1 * (dot(s, keep1) - 2.0 * t)) + u
    v = inverse_norm(colsq1) * second_ref[width : 2 * width]
    e = second_ref[:width] + dot(keep1, v)
    f = dot_short(q, second_ref[2 * width :])
    mixed = dot_short(jnp.concatenate([p, q], axis=0), jnp.concatenate([e, v], axis=1))
    a0 = mixed[:width, :width] + dot_short(keep0, f)
    a1 = -(mixed[width:, :width] + mixed[:width, width:] + f)
    a2 = mixed[width:, width:]
    none = jnp.zeros_like(a0)
    spread = jnp.concatenate(
        [
            jnp.concatenate([a0, none], axis=1),
            jnp.concatenate([a1, a0], axis=1),
            jnp.concatenate([a2, a1], axis=1),
            jnp.concatenate([none, a2], axis=1),
        ],
        axis=0,
    )
    basis = jnp.concatenate([x_ref[...], z1_ref[...], z2_ref[...], z3_ref[...]], axis=1)
    result = dot_short(basis, spread)
    block_ref[...] = result[:, :width]
    image_ref[...] = result[:, :width] - result[:, width:]


def finish(index, x, z1, z2, z3, first, second, near, far, pieces, verts_all):
    out = jax.ShapeDtypeStruct(x.shape, jnp.float32)
    width = x.shape[1]
    return pl.pallas_call(
        functools.partial(finish_kernel, pieces, verts_all),
        out_shape=[out, out],
        in_specs=smem(1) + vmem(8),
        out_specs=vmem(2),
        scratch_shapes=[pltpu.VMEM((5, width, width), jnp.float32)],
        compiler_params=pltpu.CompilerParams(vmem_limit_bytes=4 * VMEM_BYTES),
        name="finish",
    )(index, x, z1, z2, z3, first, second, near, far)


def split(array):
    high = lax.reduce_precision(array, 8, 7)
    return jnp.concatenate([high, array - high]).astype(jnp.bfloat16)


def join(coded):
    high, low = jnp.split(coded.astype(jnp.float32), 2)
    return high + low


def local(
    start_block,
    vertex_scale,
    adj_tiles,
    tile_row,
    tile_col,
    live_count,
    rotation_first,
    rotation_second,
):
    n_row, n_col = lax.axis_size("row"), lax.axis_size("col")
    row_at, col_at = lax.axis_index("row"), lax.axis_index("col")
    sub = start_block.shape[0]
    verts_all = sub * n_row * n_col
    tiles = adj_tiles[0, 0]
    halves = sub // tiles.shape[1]
    slots = jnp.arange(tiles.shape[0], dtype=jnp.int32)
    cols = ((tile_col[0, 0] // halves) ^ col_at) * halves + tile_col[0, 0] % halves
    rows = ((tile_row[0, 0] // halves) ^ row_at) * halves + tile_row[0, 0] % halves
    width = start_block.shape[1]
    inner = [("col", m) for m in range(2, n_col, 2)]
    outer = [("row", k) for k in range(1, n_row)]
    place = 2 * row_at + col_at % 2
    packed = (width // (2 * n_row)) % 8 == 0
    if not packed:
        inner, outer, place = outer, inner, col_at
    cols, rows, index = lax.optimization_barrier((cols, rows, place.reshape(1)))
    dense = None
    if 2 * n_row * n_col * sub * sub <= DENSE_BYTES:
        dense = place_tiles(live_count[0], cols, rows, tiles, n_row * sub, n_col * sub)
    else:
        rows = jnp.where(slots < live_count[0, 0], rows, n_row * halves)
    scale = vertex_scale[:, None]

    def spread(block):
        own = (scale * block).astype(jnp.bfloat16)
        return [own] + [swap(own, "col", m) for m in range(2, n_col, 2)]

    def twin(near):
        return [swap(piece, "col", 1) for piece in near]

    def multiply(near, far):
        pieces = [piece for pair in zip(near, far) for piece in pair]
        if dense is None:
            return tile_products(cols, rows, tiles, pieces, n_row)
        return dense_products(dense, pieces, n_row)

    def send(parts, extra=None):
        if extra is None:
            return [parts[0]] + [swap(parts[k], "row", k) for k in range(1, n_row)], []
        arrived = [
            swap(jnp.concatenate([parts[k], extra[k]]), "row", k) for k in range(1, n_row)
        ]
        return [parts[0]] + [part[:sub] for part in arrived], [part[sub:] for part in arrived]

    def collect(parts):
        summed = parts[0]
        for part in parts[1:]:
            summed = summed + part.astype(jnp.float32)
        return scale * summed

    def cut_grams(x, z1, z2):
        near, far = grams(index, x, z1, z2, 2 * (len(outer) + 1))
        near = near + swap(far, "col", 1)
        return [near[q] for q in range(len(outer) + 1)]

    def add(mine, arrived):
        for piece in arrived:
            mine = mine + piece
        return mine

    near = spread(start_block)
    if dense is not None:
        near[0], dense = lax.optimization_barrier((near[0], dense))
    z1 = collect(send(multiply(near, twin(near)))[0])
    near = spread(z1)
    z2 = collect(send(multiply(near, twin(near)))[0])
    gram = cut_grams(start_block, z1, z2)
    near = spread(z2)
    gram = add(gram[0], [swap(gram[q + 1], *hop) for q, hop in enumerate(outer)])
    gram = add(gram, [swap(gram, *hop) for hop in inner])
    parts = multiply(near, twin(near))
    if packed:
        parts, arrived = send(parts, [split(gram)] * n_row)
        arrived = [join(piece) for piece in arrived]
    else:
        parts, _ = send(parts)
        arrived = [swap(gram, *hop) for hop in outer]
    z3 = collect(parts)
    gram_near = jnp.stack([gram] + arrived)
    gram_far = swap(gram_near, "col", 1)
    return tuple(
        finish(
            index,
            start_block,
            z1,
            z2,
            z3,
            rotation_first,
            rotation_second,
            gram_near,
            gram_far,
            2 * gram_near.shape[0],
            verts_all,
        )
    )


def solution(mesh):
    placed = (
        P(("row", "col"), None),
        P(("row", "col")),
        P("row", "col", None, None, None),
        P("row", "col", None),
        P("row", "col", None),
        P("row", "col"),
        P(),
        P(),
    )
    return jax.shard_map(
        local,
        mesh=mesh,
        in_specs=placed,
        out_specs=(P(("row", "col"), None), P(("row", "col"), None)),
        check_vma=False,
    )
```

```python
import functools

import jax
import jax.numpy as jnp
from jax import lax
from jax.experimental import pallas as pl
from jax.experimental.pallas import tpu as pltpu
from jax.sharding import PartitionSpec as P

HIGH = lax.Precision.HIGHEST
VMEM_BYTES = 2 * 1024 * 1024
DENSE_BYTES = 8 * 1024 * 1024


def swap(array, axis, mask):
    size = lax.axis_size(axis)
    return lax.ppermute(array, axis, [(k, k ^ mask) for k in range(size)])


def vmem(count):
    return [pl.BlockSpec(memory_space=pltpu.VMEM)] * count


def smem(count):
    return [pl.BlockSpec(memory_space=pltpu.SMEM)] * count


def dot(left, right, contract=((1,), (0,))):
    return lax.dot_general(
        left, right, (contract, ((), ())), precision=HIGH, preferred_element_type=jnp.float32
    )


def dot_short(left, right):
    left_high, right_high = left.astype(jnp.bfloat16), right.astype(jnp.bfloat16)
    left_low = (left - left_high.astype(jnp.float32)).astype(jnp.bfloat16)
    right_low = (right - right_high.astype(jnp.float32)).astype(jnp.bfloat16)
    return jnp.dot(
        jnp.concatenate([left_low, left_high, left_high], axis=1),
        jnp.concatenate([right_high, right_low, right_high], axis=0),
        preferred_element_type=jnp.float32,
    )


def tiles_kernel(n_col, n_row, unroll, cols_ref, rows_ref, tiles_ref, *refs):
    pieces, outs = refs[:n_col], refs[n_col : n_col + n_row]
    panel, total = refs[n_col + n_row :]
    sub = pieces[0].shape[0]
    slots, side = tiles_ref.shape[0], tiles_ref.shape[1]
    for m, piece in enumerate(pieces):
        panel[m * sub : (m + 1) * sub] = piece[...]
    total[...] = jnp.zeros_like(total)

    def step(group, carry):
        products = []
        for u in range(unroll):
            slot = group * unroll + u
            column = pl.multiple_of(cols_ref[slot] * side, side)
            products.append(
                jnp.dot(
                    tiles_ref[slot],
                    panel[pl.ds(column, side), :],
                    preferred_element_type=jnp.float32,
                )
            )
        for u in range(unroll):
            row = pl.multiple_of(rows_ref[group * unroll + u] * side, side)
            total[pl.ds(row, side), :] += products[u]
        return carry

    lax.fori_loop(0, slots // unroll, step, 0)
    outs[0][...] = total[:sub]
    for k in range(1, n_row):
        outs[k][...] = total[k * sub : (k + 1) * sub].astype(outs[k].dtype)


def tile_products(cols, rows, tiles, pieces, n_row):
    n_col = len(pieces)
    sub, width = pieces[0].shape
    slots, side = tiles.shape[0], tiles.shape[1]
    unroll = 4 if slots % 4 == 0 else 1
    return pl.pallas_call(
        functools.partial(tiles_kernel, n_col, n_row, unroll),
        out_shape=[
            jax.ShapeDtypeStruct((sub, width), jnp.float32 if k == 0 else jnp.bfloat16)
            for k in range(n_row)
        ],
        in_specs=smem(2) + vmem(1 + n_col),
        out_specs=vmem(n_row),
        scratch_shapes=[
            pltpu.VMEM((n_col * sub, width), jnp.bfloat16),
            pltpu.VMEM((n_row * sub + side, width), jnp.float32),
        ],
        compiler_params=pltpu.CompilerParams(vmem_limit_bytes=8 * VMEM_BYTES),
        cost_estimate=pl.CostEstimate(
            flops=2 * slots * side * side * width,
            bytes_accessed=2 * slots * side * side,
            transcendentals=0,
        ),
        name="tile_products",
    )(cols, rows, tiles, *pieces)


def place_kernel(count_ref, cols_ref, rows_ref, tiles_ref, dense_ref):
    side = tiles_ref.shape[1]
    dense_ref[...] = jnp.zeros_like(dense_ref)

    def step(slot, carry):
        row = pl.multiple_of(rows_ref[slot] * side, side)
        column = pl.multiple_of(cols_ref[slot] * side, side)
        at = (pl.ds(row, side), pl.ds(column, side))
        total = dense_ref[at].astype(jnp.float32) + tiles_ref[slot].astype(jnp.float32)
        dense_ref[at] = total.astype(dense_ref.dtype)
        return carry

    lax.fori_loop(0, jnp.minimum(count_ref[0], tiles_ref.shape[0]), step, 0)


def place_tiles(count, cols, rows, tiles, height, width):
    return pl.pallas_call(
        place_kernel,
        out_shape=jax.ShapeDtypeStruct((height, width), jnp.bfloat16),
        in_specs=smem(3) + vmem(1),
        out_specs=vmem(1)[0],
        compiler_params=pltpu.CompilerParams(vmem_limit_bytes=VMEM_BYTES),
        cost_estimate=pl.CostEstimate(
            flops=0, bytes_accessed=4 * height * width, transcendentals=0
        ),
        name="place_tiles",
    )(count, cols, rows, tiles)


def near_kernel(dense_ref, *refs):
    pieces, total_ref, panel = refs[:-2], refs[-2], refs[-1]
    sub = pieces[0].shape[0]
    for m, piece in enumerate(pieces):
        panel[m * sub : (m + 1) * sub] = piece[...]
    for at in range(0, total_ref.shape[0], sub):
        total_ref[at : at + sub] = jnp.dot(
            dense_ref[at : at + sub, : len(pieces) * sub],
            panel[...],
            preferred_element_type=jnp.float32,
        )


def far_kernel(dense_ref, total_ref, *refs):
    count = (len(refs) - 1) - total_ref.shape[0] // refs[0].shape[0]
    pieces, outs, panel = refs[:count], refs[count:-1], refs[-1]
    sub = pieces[0].shape[0]
    for m, piece in enumerate(pieces):
        panel[m * sub : (m + 1) * sub] = piece[...]
    for k, out in enumerate(outs):
        part = total_ref[k * sub : (k + 1) * sub] + jnp.dot(
            dense_ref[k * sub : (k + 1) * sub, count * sub :],
            panel[...],
            preferred_element_type=jnp.float32,
        )
        out[...] = part.astype(out.dtype)


def near_products(dense, near):
    sub, width = near[0].shape
    return pl.pallas_call(
        near_kernel,
        out_shape=jax.ShapeDtypeStruct((dense.shape[0], width), jnp.float32),
        in_specs=vmem(1 + len(near)),
        out_specs=vmem(1)[0],
        scratch_shapes=[pltpu.VMEM((len(near) * sub, width), jnp.bfloat16)],
        compiler_params=pltpu.CompilerParams(vmem_limit_bytes=VMEM_BYTES),
        cost_estimate=pl.CostEstimate(
            flops=dense.size * width, bytes_accessed=dense.size, transcendentals=0
        ),
        name="near_products",
    )(dense, *near)


def far_products(dense, total, far):
    sub, width = far[0].shape
    n_row = dense.shape[0] // sub
    return pl.pallas_call(
        far_kernel,
        out_shape=[
            jax.ShapeDtypeStruct((sub, width), jnp.float32 if k == 0 else jnp.bfloat16)
            for k in range(n_row)
        ],
        in_specs=vmem(2 + len(far)),
        out_specs=vmem(n_row),
        scratch_shapes=[pltpu.VMEM((len(far) * sub, width), jnp.bfloat16)],
        compiler_params=pltpu.CompilerParams(vmem_limit_bytes=VMEM_BYTES),
        cost_estimate=pl.CostEstimate(
            flops=dense.size * width, bytes_accessed=dense.size, transcendentals=0
        ),
        name="far_products",
    )(dense, total, *far)


def indices(width):
    return (
        lax.broadcasted_iota(jnp.int32, (width, width), 0),
        lax.broadcasted_iota(jnp.int32, (width, width), 1),
    )


def column_sum(array):
    return jnp.sum(array, axis=0, keepdims=True)


def early_kernel(x_ref, z1_ref, out_ref):
    x, z1 = x_ref[...], z1_ref[...]
    row, col = indices(x.shape[1])
    eye = (row == col).astype(jnp.float32)
    out_ref[0] = dot(x, x, ((0,), (0,))) - x.shape[0] * eye
    out_ref[1] = dot(x, z1, ((0,), (0,)))
    out_ref[2] = dot(z1, z1, ((0,), (0,)))


def early_grams(x, z1):
    width = x.shape[1]
    return pl.pallas_call(
        early_kernel,
        out_shape=jax.ShapeDtypeStruct((3, width, width), jnp.float32),
        in_specs=vmem(2),
        out_specs=vmem(1)[0],
        compiler_params=pltpu.CompilerParams(vmem_limit_bytes=4 * VMEM_BYTES),
        name="early_grams",
    )(x, z1)


def gram_kernel(pieces, index_ref, early_ref, x_ref, z1_ref, z2_ref, near_ref, far_ref, whole):
    z2 = z2_ref[...]
    width = z2.shape[1]
    row, col = indices(width)
    eye = (row == col).astype(jnp.float32)
    n00, n11 = early_ref[0], early_ref[2]
    side = jnp.concatenate([x_ref[...], z1_ref[...], z2], axis=1)
    late = dot_short(side.T, z2)
    diagonal = column_sum(eye * n11)
    last = jnp.where((row == width - 2) & (col == 0), n11[width - 1 :, width - 1 :], 0.0)
    whole[0] = jnp.where(row <= col, n00, n11)
    whole[1] = jnp.where(
        row <= col, late[2 * width :], jnp.where(row == width - 1, diagonal, last)
    )
    whole[2] = early_ref[1]
    whole[3] = late[:width]
    whole[4] = late[width : 2 * width]
    rows = width // pieces
    for m in range(pieces):
        out = far_ref if m % 2 else near_ref
        start = pl.multiple_of((index_ref[0] ^ m) * rows, rows)
        for at in range(whole.shape[0]):
            out[m // 2, at * rows : (at + 1) * rows] = whole[at, pl.ds(start, rows), :]


def grams(index, early, x, z1, z2, pieces):
    width = x.shape[1]
    cut = jax.ShapeDtypeStruct((pieces // 2, 5 * (width // pieces), width), jnp.float32)
    return pl.pallas_call(
        functools.partial(gram_kernel, pieces),
        out_shape=[cut, cut],
        in_specs=smem(1) + vmem(4),
        out_specs=vmem(2),
        scratch_shapes=[pltpu.VMEM((5, width, width), jnp.float32)],
        compiler_params=pltpu.CompilerParams(vmem_limit_bytes=4 * VMEM_BYTES),
        name="grams",
    )(index, early, x, z1, z2)


def finish_kernel(
    pieces,
    verts_all,
    index_ref,
    x_ref,
    z1_ref,
    z2_ref,
    z3_ref,
    first_ref,
    second_ref,
    near_ref,
    far_ref,
    block_ref,
    image_ref,
    whole,
):
    width = x_ref.shape[1]
    rows = width // pieces
    for m in range(pieces):
        piece = far_ref if m % 2 else near_ref
        start = pl.multiple_of((index_ref[0] ^ m) * rows, rows)
        for at in range(whole.shape[0]):
            whole[at, pl.ds(start, rows), :] = piece[m // 2, at * rows : (at + 1) * rows]
    row, col = indices(width)
    eye = (row == col).astype(jnp.float32)
    first, third, n01, n02, n12 = (whole[at] for at in range(5))
    first_t = first.T
    diagonal = jnp.where(
        col[:1] == width - 1, third[width - 2 : width - 1, :1], third[width - 1 :, :]
    )
    excess = jnp.where(row <= col, first, first_t)
    n11 = jnp.where(row > col, first, jnp.where(row < col, first_t, diagonal))
    n22 = jnp.where(row <= col, third, third.T)
    n10, n21 = n01.T, n12.T
    scale = 1.0 / verts_all

    def inverse_norm(colsq):
        norm = lax.rsqrt(jnp.maximum(colsq, 0.0) * scale + 1e-06)
        return jnp.sum(eye * norm, axis=1, keepdims=True)

    keep0 = (n01 - excess) * scale
    colsq0 = column_sum(
        keep0 * (verts_all * keep0 + dot_short(excess, keep0) - 2.0 * n01) + eye * n11
    )
    q = inverse_norm(colsq0) * first_ref[width:]
    p = first_ref[:width] + dot_short(keep0, q)
    square = dot(p, p, ((0,), (0,)))
    coeff = jnp.concatenate([p, -q], axis=0)
    blocks = jnp.concatenate(
        [
            jnp.concatenate([excess, n01], axis=1),
            jnp.concatenate([n10, n11], axis=1),
            jnp.concatenate([n01, n02], axis=1),
            jnp.concatenate([n11, n12], axis=1),
            jnp.concatenate([n21, n22], axis=1),
        ],
        axis=0,
    )
    applied = dot_short(blocks, coeff)
    pair = jnp.concatenate(
        [applied[: 2 * width], applied[2 * width : 4 * width]], axis=1
    )
    both = dot_short(coeff.T, pair)
    s, t = both[:, :width] * scale, both[:, width:] * scale
    u = column_sum(coeff * applied[3 * width :]) * scale
    keep1 = (eye - square) - (s - t)
    s = s + square
    colsq1 = column_sum(keep1 * (dot_short(s, keep1) - 2.0 * t)) + u
    v = inverse_norm(colsq1 * verts_all) * second_ref[width : 2 * width]
    e = second_ref[:width] + dot_short(keep1, v)
    f = dot_short(q, second_ref[2 * width :])
    mixed = dot_short(jnp.concatenate([p, q], axis=0), jnp.concatenate([e, v], axis=1))
    a0 = mixed[:width, :width] + dot_short(keep0, f)
    a1 = -(mixed[width:, :width] + mixed[:width, width:] + f)
    a2 = mixed[width:, width:]
    none = jnp.zeros_like(a0)
    spread = jnp.concatenate(
        [
            jnp.concatenate([a0, none], axis=1),
            jnp.concatenate([a1, a0], axis=1),
            jnp.concatenate([a2, a1], axis=1),
            jnp.concatenate([none, a2], axis=1),
        ],
        axis=0,
    )
    basis = jnp.concatenate([x_ref[...], z1_ref[...], z2_ref[...], z3_ref[...]], axis=1)
    result = dot_short(basis, spread)
    block_ref[...] = result[:, :width]
    image_ref[...] = result[:, :width] - result[:, width:]


def finish(index, x, z1, z2, z3, first, second, near, far, pieces, verts_all):
    out = jax.ShapeDtypeStruct(x.shape, jnp.float32)
    width = x.shape[1]
    return pl.pallas_call(
        functools.partial(finish_kernel, pieces, verts_all),
        out_shape=[out, out],
        in_specs=smem(1) + vmem(8),
        out_specs=vmem(2),
        scratch_shapes=[pltpu.VMEM((5, width, width), jnp.float32)],
        compiler_params=pltpu.CompilerParams(vmem_limit_bytes=4 * VMEM_BYTES),
        name="finish",
    )(index, x, z1, z2, z3, first, second, near, far)


def split(array):
    high = lax.reduce_precision(array, 8, 7)
    return jnp.concatenate([high, array - high]).astype(jnp.bfloat16)


def join(coded):
    high, low = jnp.split(coded.astype(jnp.float32), 2)
    return high + low


def local(
    start_block,
    vertex_scale,
    adj_tiles,
    tile_row,
    tile_col,
    live_count,
    rotation_first,
    rotation_second,
):
    n_row, n_col = lax.axis_size("row"), lax.axis_size("col")
    row_at, col_at = lax.axis_index("row"), lax.axis_index("col")
    sub = start_block.shape[0]
    verts_all = sub * n_row * n_col
    tiles = adj_tiles[0, 0]
    halves = sub // tiles.shape[1]
    slots = jnp.arange(tiles.shape[0], dtype=jnp.int32)
    distance = (tile_col[0, 0] // halves) ^ col_at
    place = (distance % 2 + 1) * (n_col // 2) - 1 - distance // 2
    cols = place * halves + tile_col[0, 0] % halves
    rows = ((tile_row[0, 0] // halves) ^ row_at) * halves + tile_row[0, 0] % halves
    width = start_block.shape[1]
    inner = [("col", m) for m in range(2, n_col, 2)]
    outer = [("row", k) for k in range(1, n_row)]
    place = 2 * row_at + col_at % 2
    packed = (width // (2 * n_row)) % 8 == 0
    if not packed:
        inner, outer, place = outer, inner, col_at
    cols, rows, index = lax.optimization_barrier((cols, rows, place.reshape(1)))
    dense = None
    if 2 * n_row * n_col * sub * sub <= DENSE_BYTES:
        dense = place_tiles(live_count[0], cols, rows, tiles, n_row * sub, n_col * sub)
    else:
        rows = jnp.where(slots < live_count[0, 0], rows, n_row * halves)
    scale = vertex_scale[:, None]

    def spread(block):
        own = (scale * block).astype(jnp.bfloat16)
        return [own] + [swap(own, "col", m) for m in range(2, n_col, 2)]

    def twin(near):
        return [swap(piece, "col", 1) for piece in near]

    def multiply(near, far):
        if dense is None:
            return tile_products(cols, rows, tiles, near[::-1] + far[::-1], n_row)
        return far_products(dense, near_products(dense, near[::-1]), far[::-1])

    def send(parts, extra=None):
        if extra is None:
            return [parts[0]] + [swap(parts[k], "row", k) for k in range(1, n_row)], []
        arrived = [
            swap(jnp.concatenate([parts[k], extra[k]]), "row", k) for k in range(1, n_row)
        ]
        return [parts[0]] + [part[:sub] for part in arrived], [part[sub:] for part in arrived]

    def collect(parts):
        summed = parts[0]
        for part in parts[1:]:
            summed = summed + part.astype(jnp.float32)
        return scale * summed

    def cut_grams(early, x, z1, z2):
        near, far = grams(index, early, x, z1, z2, 2 * (len(outer) + 1))
        near = near + swap(far, "col", 1)
        return [near[q] for q in range(len(outer) + 1)]

    def add(mine, arrived):
        for piece in arrived:
            mine = mine + piece
        return mine

    near = spread(start_block)
    if dense is not None:
        near[0], dense = lax.optimization_barrier((near[0], dense))
    z1 = collect(send(multiply(near, twin(near)))[0])
    near = spread(z1)
    early = early_grams(start_block, z1)
    z2 = collect(send(multiply(near, twin(near)))[0])
    gram = cut_grams(early, start_block, z1, z2)
    near = spread(z2)
    gram = add(gram[0], [swap(gram[q + 1], *hop) for q, hop in enumerate(outer)])
    gram = add(gram, [swap(gram, *hop) for hop in inner])
    parts = multiply(near, twin(near))
    if packed:
        parts, arrived = send(parts, [split(gram)] * n_row)
        arrived = [join(piece) for piece in arrived]
    else:
        parts, _ = send(parts)
        arrived = [swap(gram, *hop) for hop in outer]
    z3 = collect(parts)
    gram_near = jnp.stack([gram] + arrived)
    gram_far = swap(gram_near, "col", 1)
    return tuple(
        finish(
            index,
            start_block,
            z1,
            z2,
            z3,
            rotation_first,
            rotation_second,
            gram_near,
            gram_far,
            2 * gram_near.shape[0],
            verts_all,
        )
    )


def solution(mesh):
    placed = (
        P(("row", "col"), None),
        P(("row", "col")),
        P("row", "col", None, None, None),
        P("row", "col", None),
        P("row", "col", None),
        P("row", "col"),
        P(),
        P(),
    )
    return jax.shard_map(
        local,
        mesh=mesh,
        in_specs=placed,
        out_specs=(P(("row", "col"), None), P(("row", "col"), None)),
        check_vma=False,
    )
```

```python
import functools

import jax
import jax.numpy as jnp
from jax import lax
from jax.experimental import pallas as pl
from jax.experimental.pallas import tpu as pltpu
from jax.sharding import PartitionSpec as P

HIGH = lax.Precision.HIGHEST
VMEM_BYTES = 2 * 1024 * 1024
DENSE_BYTES = 8 * 1024 * 1024


def swap(array, axis, mask):
    size = lax.axis_size(axis)
    return lax.ppermute(array, axis, [(k, k ^ mask) for k in range(size)])


def vmem(count):
    return [pl.BlockSpec(memory_space=pltpu.VMEM)] * count


def smem(count):
    return [pl.BlockSpec(memory_space=pltpu.SMEM)] * count


def dot(left, right, contract=((1,), (0,))):
    return lax.dot_general(
        left, right, (contract, ((), ())), precision=HIGH, preferred_element_type=jnp.float32
    )


def dot_short(left, right):
    left_high, right_high = left.astype(jnp.bfloat16), right.astype(jnp.bfloat16)
    left_low = (left - left_high.astype(jnp.float32)).astype(jnp.bfloat16)
    right_low = (right - right_high.astype(jnp.float32)).astype(jnp.bfloat16)
    return jnp.dot(
        jnp.concatenate([left_low, left_high, left_high], axis=1),
        jnp.concatenate([right_high, right_low, right_high], axis=0),
        preferred_element_type=jnp.float32,
    )


def tiles_kernel(n_col, n_row, unroll, cols_ref, rows_ref, tiles_ref, *refs):
    pieces, outs = refs[:n_col], refs[n_col : n_col + n_row]
    panel, total = refs[n_col + n_row :]
    sub = pieces[0].shape[0]
    slots, side = tiles_ref.shape[0], tiles_ref.shape[1]
    for m, piece in enumerate(pieces):
        panel[m * sub : (m + 1) * sub] = piece[...]
    total[...] = jnp.zeros_like(total)

    def step(group, carry):
        products = []
        for u in range(unroll):
            slot = group * unroll + u
            column = pl.multiple_of(cols_ref[slot] * side, side)
            products.append(
                jnp.dot(
                    tiles_ref[slot],
                    panel[pl.ds(column, side), :],
                    preferred_element_type=jnp.float32,
                )
            )
        for u in range(unroll):
            row = pl.multiple_of(rows_ref[group * unroll + u] * side, side)
            total[pl.ds(row, side), :] += products[u]
        return carry

    lax.fori_loop(0, slots // unroll, step, 0)
    outs[0][...] = total[:sub]
    for k in range(1, n_row):
        outs[k][...] = total[k * sub : (k + 1) * sub].astype(outs[k].dtype)


def tile_products(cols, rows, tiles, pieces, n_row):
    n_col = len(pieces)
    sub, width = pieces[0].shape
    slots, side = tiles.shape[0], tiles.shape[1]
    unroll = 4 if slots % 4 == 0 else 1
    return pl.pallas_call(
        functools.partial(tiles_kernel, n_col, n_row, unroll),
        out_shape=[
            jax.ShapeDtypeStruct((sub, width), jnp.float32 if k == 0 else jnp.bfloat16)
            for k in range(n_row)
        ],
        in_specs=smem(2) + vmem(1 + n_col),
        out_specs=vmem(n_row),
        scratch_shapes=[
            pltpu.VMEM((n_col * sub, width), jnp.bfloat16),
            pltpu.VMEM((n_row * sub + side, width), jnp.float32),
        ],
        compiler_params=pltpu.CompilerParams(vmem_limit_bytes=8 * VMEM_BYTES),
        cost_estimate=pl.CostEstimate(
            flops=2 * slots * side * side * width,
            bytes_accessed=2 * slots * side * side,
            transcendentals=0,
        ),
        name="tile_products",
    )(cols, rows, tiles, *pieces)


def place_kernel(count_ref, cols_ref, rows_ref, tiles_ref, dense_ref):
    side = tiles_ref.shape[1]
    dense_ref[...] = jnp.zeros_like(dense_ref)

    def step(slot, carry):
        row = pl.multiple_of(rows_ref[slot] * side, side)
        column = pl.multiple_of(cols_ref[slot] * side, side)
        at = (pl.ds(row, side), pl.ds(column, side))
        total = dense_ref[at].astype(jnp.float32) + tiles_ref[slot].astype(jnp.float32)
        dense_ref[at] = total.astype(dense_ref.dtype)
        return carry

    lax.fori_loop(0, jnp.minimum(count_ref[0], tiles_ref.shape[0]), step, 0)


def place_tiles(count, cols, rows, tiles, height, width):
    return pl.pallas_call(
        place_kernel,
        out_shape=jax.ShapeDtypeStruct((height, width), jnp.bfloat16),
        in_specs=smem(3) + vmem(1),
        out_specs=vmem(1)[0],
        compiler_params=pltpu.CompilerParams(vmem_limit_bytes=VMEM_BYTES),
        cost_estimate=pl.CostEstimate(
            flops=0, bytes_accessed=4 * height * width, transcendentals=0
        ),
        name="place_tiles",
    )(count, cols, rows, tiles)


def near_kernel(dense_ref, *refs):
    pieces, total_ref, panel = refs[:-2], refs[-2], refs[-1]
    sub = pieces[0].shape[0]
    for m, piece in enumerate(pieces):
        panel[m * sub : (m + 1) * sub] = piece[...]
    for at in range(0, total_ref.shape[0], sub):
        total_ref[at : at + sub] = jnp.dot(
            dense_ref[at : at + sub, : len(pieces) * sub],
            panel[...],
            preferred_element_type=jnp.float32,
        )


def far_kernel(dense_ref, total_ref, *refs):
    count = (len(refs) - 1) - total_ref.shape[0] // refs[0].shape[0]
    pieces, outs, panel = refs[:count], refs[count:-1], refs[-1]
    sub = pieces[0].shape[0]
    for m, piece in enumerate(pieces):
        panel[m * sub : (m + 1) * sub] = piece[...]
    for k, out in enumerate(outs):
        part = total_ref[k * sub : (k + 1) * sub] + jnp.dot(
            dense_ref[k * sub : (k + 1) * sub, count * sub :],
            panel[...],
            preferred_element_type=jnp.float32,
        )
        out[...] = part.astype(out.dtype)


def near_products(dense, near):
    sub, width = near[0].shape
    return pl.pallas_call(
        near_kernel,
        out_shape=jax.ShapeDtypeStruct((dense.shape[0], width), jnp.float32),
        in_specs=vmem(1 + len(near)),
        out_specs=vmem(1)[0],
        scratch_shapes=[pltpu.VMEM((len(near) * sub, width), jnp.bfloat16)],
        compiler_params=pltpu.CompilerParams(vmem_limit_bytes=VMEM_BYTES),
        cost_estimate=pl.CostEstimate(
            flops=dense.size * width, bytes_accessed=dense.size, transcendentals=0
        ),
        name="near_products",
    )(dense, *near)


def far_products(dense, total, far):
    sub, width = far[0].shape
    n_row = dense.shape[0] // sub
    return pl.pallas_call(
        far_kernel,
        out_shape=[
            jax.ShapeDtypeStruct((sub, width), jnp.float32 if k == 0 else jnp.bfloat16)
            for k in range(n_row)
        ],
        in_specs=vmem(2 + len(far)),
        out_specs=vmem(n_row),
        scratch_shapes=[pltpu.VMEM((len(far) * sub, width), jnp.bfloat16)],
        compiler_params=pltpu.CompilerParams(vmem_limit_bytes=VMEM_BYTES),
        cost_estimate=pl.CostEstimate(
            flops=dense.size * width, bytes_accessed=dense.size, transcendentals=0
        ),
        name="far_products",
    )(dense, total, *far)


def indices(width):
    return (
        lax.broadcasted_iota(jnp.int32, (width, width), 0),
        lax.broadcasted_iota(jnp.int32, (width, width), 1),
    )


def column_sum(array):
    return jnp.sum(array, axis=0, keepdims=True)


def early_kernel(x_ref, z1_ref, out_ref):
    x, z1 = x_ref[...], z1_ref[...]
    row, col = indices(x.shape[1])
    eye = (row == col).astype(jnp.float32)
    out_ref[0] = dot(x, x, ((0,), (0,))) - x.shape[0] * eye
    out_ref[1] = dot(x, z1, ((0,), (0,)))
    out_ref[2] = dot(z1, z1, ((0,), (0,)))


def early_grams(x, z1):
    width = x.shape[1]
    return pl.pallas_call(
        early_kernel,
        out_shape=jax.ShapeDtypeStruct((3, width, width), jnp.float32),
        in_specs=vmem(2),
        out_specs=vmem(1)[0],
        compiler_params=pltpu.CompilerParams(vmem_limit_bytes=4 * VMEM_BYTES),
        name="early_grams",
    )(x, z1)


def gram_kernel(pieces, index_ref, early_ref, x_ref, z1_ref, z2_ref, near_ref, far_ref, whole):
    z2 = z2_ref[...]
    width = z2.shape[1]
    row, col = indices(width)
    eye = (row == col).astype(jnp.float32)
    n00, n11 = early_ref[0], early_ref[2]
    side = jnp.concatenate([x_ref[...], z1_ref[...], z2], axis=1)
    late = dot_short(side.T, z2)
    diagonal = column_sum(eye * n11)
    last = jnp.where((row == width - 2) & (col == 0), n11[width - 1 :, width - 1 :], 0.0)
    whole[0] = jnp.where(row <= col, n00, n11)
    whole[1] = jnp.where(
        row <= col, late[2 * width :], jnp.where(row == width - 1, diagonal, last)
    )
    whole[2] = early_ref[1]
    whole[3] = late[:width]
    whole[4] = late[width : 2 * width]
    rows = width // pieces
    for m in range(pieces):
        out = far_ref if m % 2 else near_ref
        start = pl.multiple_of((index_ref[0] ^ m) * rows, rows)
        for at in range(whole.shape[0]):
            out[m // 2, at * rows : (at + 1) * rows] = whole[at, pl.ds(start, rows), :]


def grams(index, early, x, z1, z2, pieces):
    width = x.shape[1]
    cut = jax.ShapeDtypeStruct((pieces // 2, 5 * (width // pieces), width), jnp.float32)
    return pl.pallas_call(
        functools.partial(gram_kernel, pieces),
        out_shape=[cut, cut],
        in_specs=smem(1) + vmem(4),
        out_specs=vmem(2),
        scratch_shapes=[pltpu.VMEM((5, width, width), jnp.float32)],
        compiler_params=pltpu.CompilerParams(vmem_limit_bytes=4 * VMEM_BYTES),
        name="grams",
    )(index, early, x, z1, z2)


def finish_kernel(
    pieces,
    verts_all,
    index_ref,
    x_ref,
    z1_ref,
    z2_ref,
    z3_ref,
    first_ref,
    second_ref,
    near_ref,
    far_ref,
    block_ref,
    image_ref,
    whole,
):
    width = x_ref.shape[1]
    rows = width // pieces
    for m in range(pieces):
        piece = far_ref if m % 2 else near_ref
        start = pl.multiple_of((index_ref[0] ^ m) * rows, rows)
        for at in range(whole.shape[0]):
            whole[at, pl.ds(start, rows), :] = piece[m // 2, at * rows : (at + 1) * rows]
    row, col = indices(width)
    eye = (row == col).astype(jnp.float32)
    first, third, n01, n02, n12 = (whole[at] for at in range(5))
    first_t = first.T
    diagonal = jnp.where(
        col[:1] == width - 1, third[width - 2 : width - 1, :1], third[width - 1 :, :]
    )
    excess = jnp.where(row <= col, first, first_t)
    n11 = jnp.where(row > col, first, jnp.where(row < col, first_t, diagonal))
    n22 = jnp.where(row <= col, third, third.T)
    n10, n21 = n01.T, n12.T
    scale = 1.0 / verts_all

    def inverse_norm(colsq):
        norm = lax.rsqrt(jnp.maximum(colsq, 0.0) * scale + 1e-06)
        return jnp.sum(eye * norm, axis=1, keepdims=True)

    keep0 = (n01 - excess) * scale
    second_x = second_ref[:width]
    left = jnp.concatenate([excess, n10, n01, n11, n21], axis=0)
    right = jnp.concatenate([n01, n11, n02, n12, n22], axis=0)
    ready = dot_short(left, jnp.concatenate([keep0, first_ref[:width]], axis=1))
    colsq0 = column_sum(
        keep0 * (verts_all * keep0 + ready[:width, :width] - 2.0 * n01) + eye * n11
    )
    q = inverse_norm(colsq0) * first_ref[width:]
    applied = ready[:, width:] + dot_short(ready[:, :width] - right, q)
    p = first_ref[:width] + dot_short(keep0, q)
    square = dot(p, p, ((0,), (0,)))
    coeff = jnp.concatenate([p, -q], axis=0)
    f = dot_short(q, second_ref[2 * width :])
    start = dot_short(jnp.concatenate([p, q], axis=0), second_x)
    c0 = start[:width] + dot_short(keep0, f)
    c1 = -(start[width:] + f)
    pair = jnp.concatenate(
        [applied[: 2 * width], applied[2 * width : 4 * width]], axis=1
    )
    both = dot_short(coeff.T, pair)
    s, t = both[:, :width] * scale, both[:, width:] * scale
    u = column_sum(coeff * applied[3 * width :]) * scale
    keep1 = (eye - square) - (s - t)
    s = s + square
    kept = dot_short(jnp.concatenate([s, p, q], axis=0), keep1)
    colsq1 = column_sum(keep1 * (kept[:width] - 2.0 * t)) + u
    v = inverse_norm(colsq1 * verts_all) * second_ref[width : 2 * width]
    w0, w1 = kept[width : 2 * width], -(kept[2 * width :] + p)
    none = jnp.zeros_like(c0)
    mixed = dot_short(jnp.concatenate([w0, w1, q], axis=0), v)
    a0, a1, a2 = c0 + mixed[:width], c1 + mixed[width : 2 * width], mixed[2 * width :]
    spread = jnp.concatenate(
        [
            jnp.concatenate([a0, none], axis=1),
            jnp.concatenate([a1, a0], axis=1),
            jnp.concatenate([a2, a1], axis=1),
            jnp.concatenate([none, a2], axis=1),
        ],
        axis=0,
    )
    basis = jnp.concatenate([x_ref[...], z1_ref[...], z2_ref[...], z3_ref[...]], axis=1)
    result = dot_short(basis, spread)
    block_ref[...] = result[:, :width]
    image_ref[...] = result[:, :width] - result[:, width:]


def finish(index, x, z1, z2, z3, first, second, near, far, pieces, verts_all):
    out = jax.ShapeDtypeStruct(x.shape, jnp.float32)
    width = x.shape[1]
    return pl.pallas_call(
        functools.partial(finish_kernel, pieces, verts_all),
        out_shape=[out, out],
        in_specs=smem(1) + vmem(8),
        out_specs=vmem(2),
        scratch_shapes=[pltpu.VMEM((5, width, width), jnp.float32)],
        compiler_params=pltpu.CompilerParams(vmem_limit_bytes=4 * VMEM_BYTES),
        name="finish",
    )(index, x, z1, z2, z3, first, second, near, far)


def split(array):
    high = lax.reduce_precision(array, 8, 7)
    return jnp.concatenate([high, array - high]).astype(jnp.bfloat16)


def join(coded):
    high, low = jnp.split(coded.astype(jnp.float32), 2)
    return high + low


def local(
    start_block,
    vertex_scale,
    adj_tiles,
    tile_row,
    tile_col,
    live_count,
    rotation_first,
    rotation_second,
):
    n_row, n_col = lax.axis_size("row"), lax.axis_size("col")
    row_at, col_at = lax.axis_index("row"), lax.axis_index("col")
    sub = start_block.shape[0]
    verts_all = sub * n_row * n_col
    tiles = adj_tiles[0, 0]
    halves = sub // tiles.shape[1]
    slots = jnp.arange(tiles.shape[0], dtype=jnp.int32)
    distance = (tile_col[0, 0] // halves) ^ col_at
    place = (distance % 2 + 1) * (n_col // 2) - 1 - distance // 2
    cols = place * halves + tile_col[0, 0] % halves
    rows = ((tile_row[0, 0] // halves) ^ row_at) * halves + tile_row[0, 0] % halves
    width = start_block.shape[1]
    inner = [("col", m) for m in range(2, n_col, 2)]
    outer = [("row", k) for k in range(1, n_row)]
    place = 2 * row_at + col_at % 2
    packed = (width // (2 * n_row)) % 8 == 0
    if not packed:
        inner, outer, place = outer, inner, col_at
    cols, rows, index = lax.optimization_barrier((cols, rows, place.reshape(1)))
    dense = None
    if 2 * n_row * n_col * sub * sub <= DENSE_BYTES:
        dense = place_tiles(live_count[0], cols, rows, tiles, n_row * sub, n_col * sub)
    else:
        rows = jnp.where(slots < live_count[0, 0], rows, n_row * halves)
    scale = vertex_scale[:, None]

    def spread(block):
        own = (scale * block).astype(jnp.bfloat16)
        return [own] + [swap(own, "col", m) for m in range(2, n_col, 2)]

    def twin(near):
        return [swap(piece, "col", 1) for piece in near]

    def multiply(near, far):
        if dense is None:
            return tile_products(cols, rows, tiles, near[::-1] + far[::-1], n_row)
        return far_products(dense, near_products(dense, near[::-1]), far[::-1])

    def send(parts, extra=None):
        if extra is None:
            return [parts[0]] + [swap(parts[k], "row", k) for k in range(1, n_row)], []
        arrived = [
            swap(jnp.concatenate([parts[k], extra[k]]), "row", k) for k in range(1, n_row)
        ]
        return [parts[0]] + [part[:sub] for part in arrived], [part[sub:] for part in arrived]

    def collect(parts):
        summed = parts[0]
        for part in parts[1:]:
            summed = summed + part.astype(jnp.float32)
        return scale * summed

    def cut_grams(early, x, z1, z2):
        near, far = grams(index, early, x, z1, z2, 2 * (len(outer) + 1))
        near = near + swap(far, "col", 1)
        return [near[q] for q in range(len(outer) + 1)]

    def add(mine, arrived):
        for piece in arrived:
            mine = mine + piece
        return mine

    near = spread(start_block)
    if dense is not None:
        near[0], dense = lax.optimization_barrier((near[0], dense))
    z1 = collect(send(multiply(near, twin(near)))[0])
    near = spread(z1)
    early = early_grams(start_block, z1)
    z2 = collect(send(multiply(near, twin(near)))[0])
    gram = cut_grams(early, start_block, z1, z2)
    near = spread(z2)
    gram = add(gram[0], [swap(gram[q + 1], *hop) for q, hop in enumerate(outer)])
    gram = add(gram, [swap(gram, *hop) for hop in inner])
    parts = multiply(near, twin(near))
    if packed:
        parts, arrived = send(parts, [split(gram)] * n_row)
        arrived = [join(piece) for piece in arrived]
    else:
        parts, _ = send(parts)
        arrived = [swap(gram, *hop) for hop in outer]
    z3 = collect(parts)
    gram_near = jnp.stack([gram] + arrived)
    gram_far = swap(gram_near, "col", 1)
    return tuple(
        finish(
            index,
            start_block,
            z1,
            z2,
            z3,
            rotation_first,
            rotation_second,
            gram_near,
            gram_far,
            2 * gram_near.shape[0],
            verts_all,
        )
    )


def solution(mesh):
    placed = (
        P(("row", "col"), None),
        P(("row", "col")),
        P("row", "col", None, None, None),
        P("row", "col", None),
        P("row", "col", None),
        P("row", "col"),
        P(),
        P(),
    )
    return jax.shard_map(
        local,
        mesh=mesh,
        in_specs=placed,
        out_specs=(P(("row", "col"), None), P(("row", "col"), None)),
        check_vma=False,
    )
```

```python
import functools

import jax
import jax.numpy as jnp
from jax import lax
from jax.experimental import pallas as pl
from jax.experimental.pallas import tpu as pltpu
from jax.sharding import PartitionSpec as P

HIGH = lax.Precision.HIGHEST
VMEM_BYTES = 2 * 1024 * 1024
DENSE_BYTES = 8 * 1024 * 1024


def swap(array, axis, mask):
    size = lax.axis_size(axis)
    return lax.ppermute(array, axis, [(k, k ^ mask) for k in range(size)])


def vmem(count):
    return [pl.BlockSpec(memory_space=pltpu.VMEM)] * count


def smem(count):
    return [pl.BlockSpec(memory_space=pltpu.SMEM)] * count


def dot(left, right, contract=((1,), (0,))):
    return lax.dot_general(
        left, right, (contract, ((), ())), precision=HIGH, preferred_element_type=jnp.float32
    )


def dot_short(left, right):
    left_high, right_high = left.astype(jnp.bfloat16), right.astype(jnp.bfloat16)
    left_low = (left - left_high.astype(jnp.float32)).astype(jnp.bfloat16)
    right_low = (right - right_high.astype(jnp.float32)).astype(jnp.bfloat16)
    return jnp.dot(
        jnp.concatenate([left_low, left_high, left_high], axis=1),
        jnp.concatenate([right_high, right_low, right_high], axis=0),
        preferred_element_type=jnp.float32,
    )


def tiles_kernel(n_col, n_row, unroll, cols_ref, rows_ref, tiles_ref, *refs):
    pieces, outs = refs[:n_col], refs[n_col : n_col + n_row]
    panel, total = refs[n_col + n_row :]
    sub = pieces[0].shape[0]
    slots, side = tiles_ref.shape[0], tiles_ref.shape[1]
    for m, piece in enumerate(pieces):
        panel[m * sub : (m + 1) * sub] = piece[...]
    total[...] = jnp.zeros_like(total)

    def step(group, carry):
        products = []
        for u in range(unroll):
            slot = group * unroll + u
            column = pl.multiple_of(cols_ref[slot] * side, side)
            products.append(
                jnp.dot(
                    tiles_ref[slot],
                    panel[pl.ds(column, side), :],
                    preferred_element_type=jnp.float32,
                )
            )
        for u in range(unroll):
            row = pl.multiple_of(rows_ref[group * unroll + u] * side, side)
            total[pl.ds(row, side), :] += products[u]
        return carry

    lax.fori_loop(0, slots // unroll, step, 0)
    outs[0][...] = total[:sub]
    for k in range(1, n_row):
        outs[k][...] = total[k * sub : (k + 1) * sub].astype(outs[k].dtype)


def tile_products(cols, rows, tiles, pieces, n_row):
    n_col = len(pieces)
    sub, width = pieces[0].shape
    slots, side = tiles.shape[0], tiles.shape[1]
    unroll = 4 if slots % 4 == 0 else 1
    return pl.pallas_call(
        functools.partial(tiles_kernel, n_col, n_row, unroll),
        out_shape=[
            jax.ShapeDtypeStruct((sub, width), jnp.float32 if k == 0 else jnp.bfloat16)
            for k in range(n_row)
        ],
        in_specs=smem(2) + vmem(1 + n_col),
        out_specs=vmem(n_row),
        scratch_shapes=[
            pltpu.VMEM((n_col * sub, width), jnp.bfloat16),
            pltpu.VMEM((n_row * sub + side, width), jnp.float32),
        ],
        compiler_params=pltpu.CompilerParams(vmem_limit_bytes=8 * VMEM_BYTES),
        cost_estimate=pl.CostEstimate(
            flops=2 * slots * side * side * width,
            bytes_accessed=2 * slots * side * side,
            transcendentals=0,
        ),
        name="tile_products",
    )(cols, rows, tiles, *pieces)


def place_kernel(count_ref, cols_ref, rows_ref, tiles_ref, dense_ref):
    side = tiles_ref.shape[1]
    dense_ref[...] = jnp.zeros_like(dense_ref)

    def step(slot, carry):
        row = pl.multiple_of(rows_ref[slot] * side, side)
        column = pl.multiple_of(cols_ref[slot] * side, side)
        at = (pl.ds(row, side), pl.ds(column, side))
        total = dense_ref[at].astype(jnp.float32) + tiles_ref[slot].astype(jnp.float32)
        dense_ref[at] = total.astype(dense_ref.dtype)
        return carry

    lax.fori_loop(0, jnp.minimum(count_ref[0], tiles_ref.shape[0]), step, 0)


def place_tiles(count, cols, rows, tiles, height, width):
    return pl.pallas_call(
        place_kernel,
        out_shape=jax.ShapeDtypeStruct((height, width), jnp.bfloat16),
        in_specs=smem(3) + vmem(1),
        out_specs=vmem(1)[0],
        compiler_params=pltpu.CompilerParams(vmem_limit_bytes=VMEM_BYTES),
        cost_estimate=pl.CostEstimate(
            flops=0, bytes_accessed=4 * height * width, transcendentals=0
        ),
        name="place_tiles",
    )(count, cols, rows, tiles)


def near_kernel(dense_ref, *refs):
    pieces, total_ref, panel = refs[:-2], refs[-2], refs[-1]
    sub = pieces[0].shape[0]
    for m, piece in enumerate(pieces):
        panel[m * sub : (m + 1) * sub] = piece[...]
    for at in range(0, total_ref.shape[0], sub):
        total_ref[at : at + sub] = jnp.dot(
            dense_ref[at : at + sub, : len(pieces) * sub],
            panel[...],
            preferred_element_type=jnp.float32,
        )


def far_kernel(dense_ref, total_ref, *refs):
    count = (len(refs) - 1) - total_ref.shape[0] // refs[0].shape[0]
    pieces, outs, panel = refs[:count], refs[count:-1], refs[-1]
    sub = pieces[0].shape[0]
    for m, piece in enumerate(pieces):
        panel[m * sub : (m + 1) * sub] = piece[...]
    for k, out in enumerate(outs):
        part = total_ref[k * sub : (k + 1) * sub] + jnp.dot(
            dense_ref[k * sub : (k + 1) * sub, count * sub :],
            panel[...],
            preferred_element_type=jnp.float32,
        )
        out[...] = part.astype(out.dtype)


def near_products(dense, near):
    sub, width = near[0].shape
    return pl.pallas_call(
        near_kernel,
        out_shape=jax.ShapeDtypeStruct((dense.shape[0], width), jnp.float32),
        in_specs=vmem(1 + len(near)),
        out_specs=vmem(1)[0],
        scratch_shapes=[pltpu.VMEM((len(near) * sub, width), jnp.bfloat16)],
        compiler_params=pltpu.CompilerParams(vmem_limit_bytes=VMEM_BYTES),
        cost_estimate=pl.CostEstimate(
            flops=dense.size * width, bytes_accessed=dense.size, transcendentals=0
        ),
        name="near_products",
    )(dense, *near)


def far_products(dense, total, far):
    sub, width = far[0].shape
    n_row = dense.shape[0] // sub
    return pl.pallas_call(
        far_kernel,
        out_shape=[
            jax.ShapeDtypeStruct((sub, width), jnp.float32 if k == 0 else jnp.bfloat16)
            for k in range(n_row)
        ],
        in_specs=vmem(2 + len(far)),
        out_specs=vmem(n_row),
        scratch_shapes=[pltpu.VMEM((len(far) * sub, width), jnp.bfloat16)],
        compiler_params=pltpu.CompilerParams(vmem_limit_bytes=VMEM_BYTES),
        cost_estimate=pl.CostEstimate(
            flops=dense.size * width, bytes_accessed=dense.size, transcendentals=0
        ),
        name="far_products",
    )(dense, total, *far)


def indices(width):
    return (
        lax.broadcasted_iota(jnp.int32, (width, width), 0),
        lax.broadcasted_iota(jnp.int32, (width, width), 1),
    )


def column_sum(array):
    return jnp.sum(array, axis=0, keepdims=True)


def early_kernel(x_ref, z1_ref, out_ref):
    x, z1 = x_ref[...], z1_ref[...]
    row, col = indices(x.shape[1])
    eye = (row == col).astype(jnp.float32)
    out_ref[0] = dot(x, x, ((0,), (0,))) - x.shape[0] * eye
    out_ref[1] = dot(x, z1, ((0,), (0,)))
    out_ref[2] = dot(z1, z1, ((0,), (0,)))


def early_grams(x, z1):
    width = x.shape[1]
    return pl.pallas_call(
        early_kernel,
        out_shape=jax.ShapeDtypeStruct((3, width, width), jnp.float32),
        in_specs=vmem(2),
        out_specs=vmem(1)[0],
        compiler_params=pltpu.CompilerParams(vmem_limit_bytes=4 * VMEM_BYTES),
        name="early_grams",
    )(x, z1)


def gram_kernel(pieces, index_ref, early_ref, x_ref, z1_ref, z2_ref, near_ref, far_ref, whole):
    z2 = z2_ref[...]
    width = z2.shape[1]
    row, col = indices(width)
    eye = (row == col).astype(jnp.float32)
    n00, n11 = early_ref[0], early_ref[2]
    side = jnp.concatenate([x_ref[...], z1_ref[...], z2], axis=1)
    late = dot_short(side.T, z2)
    diagonal = column_sum(eye * n11)
    last = jnp.where((row == width - 2) & (col == 0), n11[width - 1 :, width - 1 :], 0.0)
    whole[0] = jnp.where(row <= col, n00, n11)
    whole[1] = jnp.where(
        row <= col, late[2 * width :], jnp.where(row == width - 1, diagonal, last)
    )
    whole[2] = early_ref[1]
    whole[3] = late[:width]
    whole[4] = late[width : 2 * width]
    rows = width // pieces
    for m in range(pieces):
        out = far_ref if m % 2 else near_ref
        start = pl.multiple_of((index_ref[0] ^ m) * rows, rows)
        for at in range(whole.shape[0]):
            out[m // 2, at * rows : (at + 1) * rows] = whole[at, pl.ds(start, rows), :]


def grams(index, early, x, z1, z2, pieces):
    width = x.shape[1]
    cut = jax.ShapeDtypeStruct((pieces // 2, 5 * (width // pieces), width), jnp.float32)
    return pl.pallas_call(
        functools.partial(gram_kernel, pieces),
        out_shape=[cut, cut],
        in_specs=smem(1) + vmem(4),
        out_specs=vmem(2),
        scratch_shapes=[pltpu.VMEM((5, width, width), jnp.float32)],
        compiler_params=pltpu.CompilerParams(vmem_limit_bytes=4 * VMEM_BYTES),
        name="grams",
    )(index, early, x, z1, z2)


def finish_kernel(
    pieces,
    verts_all,
    index_ref,
    x_ref,
    z1_ref,
    z2_ref,
    z3_ref,
    first_ref,
    second_ref,
    *refs,
):
    near, far = refs[: pieces // 2], refs[pieces // 2 : pieces]
    block_ref, image_ref, whole = refs[pieces:]
    width = x_ref.shape[1]
    rows = width // pieces
    for m in range(pieces):
        piece = (far if m % 2 else near)[m // 2]
        start = pl.multiple_of((index_ref[0] ^ m) * rows, rows)
        for at in range(whole.shape[0]):
            whole[at, pl.ds(start, rows), :] = piece[at * rows : (at + 1) * rows]
    row, col = indices(width)
    eye = (row == col).astype(jnp.float32)
    first, third, n01, n02, n12 = (whole[at] for at in range(5))
    first_t = first.T
    diagonal = jnp.where(
        col[:1] == width - 1, third[width - 2 : width - 1, :1], third[width - 1 :, :]
    )
    excess = jnp.where(row <= col, first, first_t)
    n11 = jnp.where(row > col, first, jnp.where(row < col, first_t, diagonal))
    n22 = jnp.where(row <= col, third, third.T)
    n10, n21 = n01.T, n12.T
    scale = 1.0 / verts_all

    def inverse_norm(colsq):
        norm = lax.rsqrt(jnp.maximum(colsq, 0.0) * scale + 1e-06)
        return jnp.sum(eye * norm, axis=1, keepdims=True)

    keep0 = (n01 - excess) * scale
    second_x = second_ref[:width]
    left = jnp.concatenate([excess, n10, n01, n11, n21], axis=0)
    right = jnp.concatenate([n01, n11, n02, n12, n22], axis=0)
    ready = dot_short(left, jnp.concatenate([keep0, first_ref[:width]], axis=1))
    colsq0 = column_sum(
        keep0 * (verts_all * keep0 + ready[:width, :width] - 2.0 * n01) + eye * n11
    )
    q = inverse_norm(colsq0) * first_ref[width:]
    applied = ready[:, width:] + dot_short(ready[:, :width] - right, q)
    p = first_ref[:width] + dot_short(keep0, q)
    square = dot(p, p, ((0,), (0,)))
    coeff = jnp.concatenate([p, -q], axis=0)
    f = dot_short(q, second_ref[2 * width :])
    start = dot_short(jnp.concatenate([p, q], axis=0), second_x)
    c0 = start[:width] + dot_short(keep0, f)
    c1 = -(start[width:] + f)
    pair = jnp.concatenate(
        [applied[: 2 * width], applied[2 * width : 4 * width]], axis=1
    )
    both = dot_short(coeff.T, pair)
    s, t = both[:, :width] * scale, both[:, width:] * scale
    u = column_sum(coeff * applied[3 * width :]) * scale
    keep1 = (eye - square) - (s - t)
    s = s + square
    kept = dot_short(jnp.concatenate([s, p, q], axis=0), keep1)
    colsq1 = column_sum(keep1 * (kept[:width] - 2.0 * t)) + u
    v = inverse_norm(colsq1 * verts_all) * second_ref[width : 2 * width]
    w0, w1 = kept[width : 2 * width], -(kept[2 * width :] + p)
    none = jnp.zeros_like(c0)
    mixed = dot_short(jnp.concatenate([w0, w1, q], axis=0), v)
    a0, a1, a2 = c0 + mixed[:width], c1 + mixed[width : 2 * width], mixed[2 * width :]
    spread = jnp.concatenate(
        [
            jnp.concatenate([a0, none], axis=1),
            jnp.concatenate([a1, a0], axis=1),
            jnp.concatenate([a2, a1], axis=1),
            jnp.concatenate([none, a2], axis=1),
        ],
        axis=0,
    )
    basis = jnp.concatenate([x_ref[...], z1_ref[...], z2_ref[...], z3_ref[...]], axis=1)
    result = dot_short(basis, spread)
    block_ref[...] = result[:, :width]
    image_ref[...] = result[:, :width] - result[:, width:]


def finish(index, x, z1, z2, z3, first, second, near, far, pieces, verts_all):
    out = jax.ShapeDtypeStruct(x.shape, jnp.float32)
    width = x.shape[1]
    return pl.pallas_call(
        functools.partial(finish_kernel, pieces, verts_all),
        out_shape=[out, out],
        in_specs=smem(1) + vmem(6 + pieces),
        out_specs=vmem(2),
        scratch_shapes=[pltpu.VMEM((5, width, width), jnp.float32)],
        compiler_params=pltpu.CompilerParams(vmem_limit_bytes=4 * VMEM_BYTES),
        name="finish",
    )(index, x, z1, z2, z3, first, second, *near, *far)


def split(array):
    high = lax.reduce_precision(array, 8, 7)
    return jnp.concatenate([high, array - high]).astype(jnp.bfloat16)


def join(coded):
    high, low = jnp.split(coded.astype(jnp.float32), 2)
    return high + low


def local(
    start_block,
    vertex_scale,
    adj_tiles,
    tile_row,
    tile_col,
    live_count,
    rotation_first,
    rotation_second,
):
    n_row, n_col = lax.axis_size("row"), lax.axis_size("col")
    row_at, col_at = lax.axis_index("row"), lax.axis_index("col")
    sub = start_block.shape[0]
    verts_all = sub * n_row * n_col
    tiles = adj_tiles[0, 0]
    halves = sub // tiles.shape[1]
    slots = jnp.arange(tiles.shape[0], dtype=jnp.int32)
    distance = (tile_col[0, 0] // halves) ^ col_at
    place = (distance % 2 + 1) * (n_col // 2) - 1 - distance // 2
    cols = place * halves + tile_col[0, 0] % halves
    rows = ((tile_row[0, 0] // halves) ^ row_at) * halves + tile_row[0, 0] % halves
    width = start_block.shape[1]
    inner = [("col", m) for m in range(2, n_col, 2)]
    outer = [("row", k) for k in range(1, n_row)]
    place = 2 * row_at + col_at % 2
    packed = (width // (2 * n_row)) % 8 == 0
    if not packed:
        inner, outer, place = outer, inner, col_at
    cols, rows, index = lax.optimization_barrier((cols, rows, place.reshape(1)))
    dense = None
    if 2 * n_row * n_col * sub * sub <= DENSE_BYTES:
        dense = place_tiles(live_count[0], cols, rows, tiles, n_row * sub, n_col * sub)
    else:
        rows = jnp.where(slots < live_count[0, 0], rows, n_row * halves)
    scale = vertex_scale[:, None]

    def spread(block):
        own = (scale * block).astype(jnp.bfloat16)
        return [own] + [swap(own, "col", m) for m in range(2, n_col, 2)]

    def twin(near):
        return [swap(piece, "col", 1) for piece in near]

    def multiply(near, far):
        if dense is None:
            return tile_products(cols, rows, tiles, near[::-1] + far[::-1], n_row)
        return far_products(dense, near_products(dense, near[::-1]), far[::-1])

    def send(parts, extra=None):
        if extra is None:
            return [parts[0]] + [swap(parts[k], "row", k) for k in range(1, n_row)], []
        arrived = [
            swap(jnp.concatenate([parts[k], extra[k]]), "row", k) for k in range(1, n_row)
        ]
        return [parts[0]] + [part[:sub] for part in arrived], [part[sub:] for part in arrived]

    def collect(parts):
        summed = parts[0]
        for part in parts[1:]:
            summed = summed + part.astype(jnp.float32)
        return scale * summed

    def cut_grams(early, x, z1, z2):
        near, far = grams(index, early, x, z1, z2, 2 * (len(outer) + 1))
        near = near + swap(far, "col", 1)
        return [near[q] for q in range(len(outer) + 1)]

    def add(mine, arrived):
        for piece in arrived:
            mine = mine + piece
        return mine

    near = spread(start_block)
    if dense is not None:
        near[0], dense = lax.optimization_barrier((near[0], dense))
    z1 = collect(send(multiply(near, twin(near)))[0])
    near = spread(z1)
    early = early_grams(start_block, z1)
    z2 = collect(send(multiply(near, twin(near)))[0])
    gram = cut_grams(early, start_block, z1, z2)
    near = spread(z2)
    gram = add(gram[0], [swap(gram[q + 1], *hop) for q, hop in enumerate(outer)])
    gram = add(gram, [swap(gram, *hop) for hop in inner])
    parts = multiply(near, twin(near))
    if packed:
        parts, arrived = send(parts, [split(gram)] * n_row)
        arrived = [join(piece) for piece in arrived]
    else:
        parts, _ = send(parts)
        arrived = [swap(gram, *hop) for hop in outer]
    z3 = collect(parts)
    gram_near = [gram] + arrived
    rest = swap(jnp.stack(arrived[::-1]), "col", 1)
    gram_far = twin([gram]) + [rest[k] for k in range(len(arrived))][::-1]
    return tuple(
        finish(
            index,
            start_block,
            z1,
            z2,
            z3,
            rotation_first,
            rotation_second,
            gram_near,
            gram_far,
            2 * len(gram_near),
            verts_all,
        )
    )


def solution(mesh):
    placed = (
        P(("row", "col"), None),
        P(("row", "col")),
        P("row", "col", None, None, None),
        P("row", "col", None),
        P("row", "col", None),
        P("row", "col"),
        P(),
        P(),
    )
    return jax.shard_map(
        local,
        mesh=mesh,
        in_specs=placed,
        out_specs=(P(("row", "col"), None), P(("row", "col"), None)),
        check_vma=False,
    )
```
